256 devices in a mesh: lat: 32 (over z_lo, y, core), lon: 8 (over x, z_hi).
Axes of the slice: x: 4, y: 4, z: 8 (z_hi: 2, z_lo: 4; z = z_hi * 4 + z_lo), core: 2. Of those that a mesh axis runs over, the one named last changes fastest.
Arguments:
- field: float32 [128, 1440, 256], P('lat', 'lon'), may hold values from -6 to 6
- legendre: float32 [512, 720, 128], P('lat'), may hold values from -1 to 1, as said below
- shifts: int32 [128, 20], P('lat'), may hold values from -16 to 16
- psi: float32 [128, 20, 9], P('lat'), may hold values from -1.3 to 1.3
- kernel_weight: float32 [9, 32, 256], replicated, may hold values from -0.375 to 0.375
Outputs:
- coefficients: float32 [512, 720, 2, 256], P('lat', None, None, 'lon')
- convolved: float32 [128, 1440, 256], P('lat', 'lon')
The draws below stay inside these ranges and needn't reach their ends.
Inputs may be any that keep to these rules, and one draw needn't show every extreme that they name: `legendre`: zero where the degree is below the order.
All inputs are finite; a program needn't handle non-finite values.
Results may differ from the reference program's by a relative error of at most 0.0001.
Values sent between devices are 32-bit elements; how exact they have to be, the bound alone decides.
A program may use at most 128 MiB of HBM per device.

```python
import math
import jax
import jax.numpy as jnp
from jax import lax

LONGITUDES = 1440
CHANNELS = 256
ORDERS = 512
DEGREES = 720
GROUP_WIDTH = 32
KERNELS = 9
SLOTS = 20
RADIUS = 2
REACH = 16
LATITUDES = 128


def draw_legendre(key, part):
    key = jax.random.fold_in(key, 7)
    values = jax.random.uniform(key, (ORDERS, DEGREES, LATITUDES), jnp.float32, -1.0, 1.0)
    values = values * (1.7 / math.sqrt(LATITUDES * LONGITUDES))
    order_index = lax.broadcasted_iota(jnp.int32, (ORDERS, DEGREES, LATITUDES), 0)
    degree_index = lax.broadcasted_iota(jnp.int32, (ORDERS, DEGREES, LATITUDES), 1)
    return jnp.where(degree_index >= order_index, values, 0.0).astype(jnp.float32)


def with_ends(drawn, key, least, high):
    longest = drawn.shape.index(max(drawn.shape))
    spots = []
    for shift in (0, 1):
        where = [jax.random.randint(jax.random.fold_in(key, axis), (), 0, length) for axis, length in enumerate(drawn.shape)]
        where[longest] = (where[longest] + shift) % drawn.shape[longest]
        spots.append(tuple(where))
    return drawn.at[spots[0]].set(least).at[spots[1]].set(high)


def levels(stream_key, extent, cuts, smallest, largest):
    loudness, own = 1.0, jax.random.fold_in(stream_key, 6)
    for axis_at, parts in cuts:
        draws = jnp.exp(jax.random.uniform(jax.random.fold_in(own, axis_at), (parts,), jnp.float32, smallest / len(cuts), largest / len(cuts)))
        loudness = loudness * jnp.repeat(draws, extent[axis_at] // parts).reshape([-1 if axis == axis_at else 1 for axis in range(len(extent))])
    return loudness


def normal_values(key, extent, spread, reach, split=(), kind=jnp.bfloat16):
    loudness = levels(key, extent, split, -0.22, 0.18) if split else 1.0
    array = jax.random.normal(key, extent, jnp.float32) * spread * loudness
    return jnp.minimum(jnp.maximum(array, -reach), reach).astype(kind)


def setup_inputs(seed: int = 0) -> dict:
    splits = jax.random.split(jax.random.key(seed), 6)
    field = normal_values(splits[0], (LATITUDES, LONGITUDES, CHANNELS), 1.0, 6.0, ((0, 32), (1, 8)), jnp.float32)
    legendre = draw_legendre(jax.random.fold_in(splits[5], 71), 0)
    shifts = with_ends(jax.random.randint(splits[2], (LATITUDES, SLOTS), -REACH, REACH + 1), jax.random.fold_in(splits[2], 1), -REACH, REACH).astype(jnp.int32)
    psi = normal_values(splits[3], (LATITUDES, SLOTS, KERNELS), 0.22, 1.3, ((0, 32),), jnp.float32)
    kernel_weight = normal_values(splits[4], (KERNELS, GROUP_WIDTH, CHANNELS), (KERNELS * GROUP_WIDTH) ** -0.5, 0.375, (), jnp.float32)
    return {"field": field, "legendre": legendre, "shifts": shifts, "psi": psi, "kernel_weight": kernel_weight}


def reference(field, legendre, shifts, psi, kernel_weight):
    spectrum = jnp.fft.rfft(field, axis=1)[:, :ORDERS, :]
    stacked = jnp.stack([jnp.real(spectrum), jnp.imag(spectrum)], axis=2).astype(field.dtype)
    coefficients = jnp.einsum('mla,amrc->mlrc', legendre, stacked, precision=lax.Precision.HIGHEST)
    groups = CHANNELS // GROUP_WIDTH
    padded = jnp.pad(field, ((RADIUS, RADIUS), (0, 0), (0, 0)))
    columns = jnp.arange(LONGITUDES, dtype=jnp.int32)
    convolved = jnp.zeros((LATITUDES, LONGITUDES, groups, GROUP_WIDTH), field.dtype)
    for slot in range(SLOTS):
        offset = slot % (2 * RADIUS + 1)
        rows = padded[offset:offset + LATITUDES]
        where = (columns[None, :] + shifts[:, slot][:, None]) % LONGITUDES
        taken = jnp.take_along_axis(rows, where[:, :, None].astype(jnp.int32), axis=1)
        mixed = jnp.einsum('ak,kco->aco', psi[:, slot, :], kernel_weight, precision=lax.Precision.HIGHEST)
        mixed = mixed.reshape(LATITUDES, GROUP_WIDTH, groups, GROUP_WIDTH)
        convolved = convolved + jnp.einsum('ajgc,acgo->ajgo', taken.reshape(LATITUDES, LONGITUDES, groups, GROUP_WIDTH), mixed, precision=lax.Precision.HIGHEST)
    return coefficients, convolved.reshape(LATITUDES, LONGITUDES, CHANNELS)
```

```python
import jax
import jax.numpy as jnp
import ml_dtypes
import numpy as np
from jax import lax
from jax.experimental import pallas as pl
from jax.experimental.pallas import tpu as pltpu
from jax.sharding import PartitionSpec as P

LON = 1440
ORDERS = 512
SLAB = 180
PAD = 184
GW = 32
KERNELS = 9
SLOTS = 20
RADIUS = 2
REACH = 16
STRIPS = 12
SPAN = 232
MESH = pl.DeviceIdType.MESH
F32 = jnp.float32
BF16 = jnp.bfloat16
ORDER_OF = [0, 4, 8, 12, 2, 6, 10, 14, 1, 3, 5, 7, 9, 11, 13, 15]


def two_parts(table):
    table = np.asarray(table, np.float32)
    high = table.astype(ml_dtypes.bfloat16)
    low = (table - high.astype(np.float32)).astype(ml_dtypes.bfloat16)
    return np.stack([high, low])


def fourier_tables():
    even, odd = [], []
    for half in range(2):
        j = SLAB * half + np.arange(PAD)
        live = (np.arange(PAD) < SLAB).astype(np.float64)

        def rows(orders, lead):
            turn = (np.asarray(orders)[:, None] * (j[None, :] + lead)) % LON
            angle = turn * (2.0 * np.pi / LON)
            both = np.stack([np.cos(angle), -np.sin(angle)], axis=1) * live
            return both.reshape(-1, PAD)

        owner = np.arange(32)[:, None] * 16
        zero = (owner + np.arange(0, 16, 4)).reshape(-1)
        two = (owner + np.arange(2, 16, 4)).reshape(-1)
        ones = (owner + np.arange(1, 16, 2)).reshape(-1)
        even.append(two_parts(np.concatenate([rows(zero, 0), rows(two, 0)])))
        odd.append(two_parts(np.concatenate([rows(ones, 0), rows(ones, 360)], axis=1)))
    return np.stack(even), np.stack(odd)


def split(value):
    high = value.astype(BF16)
    return high, (value - high.astype(F32)).astype(BF16)


def main_kernel(
    shifts, psi, field, weight, even, odd,
    conv, lhs,
    g, e, f, pk, xr, sp, r, gh, gl, bdh, bdl, te, to, es,
    load_sem, table_sem, s1_send, s1_recv, h_send, h_recv, c_send, c_recv, s3_send, s3_recv, own_sem,
):
    lat = lax.axis_index("lat")
    lon = lax.axis_index("lon")
    x, half = lon // 2, lon % 2
    z_lo, y, core = lat // 8, (lat // 2) % 4, lat % 2
    right = lax.rem(lon + 1, 8)
    left = lax.rem(lon + 7, 8)

    load = pltpu.make_async_copy(field, g.at[pl.ds(2, 4)], load_sem)
    load.start()
    load_even = pltpu.make_async_copy(even.at[half], te, table_sem.at[0])
    load_odd = pltpu.make_async_copy(odd.at[half], to, table_sem.at[1])
    load_even.start()
    load_odd.start()

    barrier = pltpu.get_barrier_semaphore()

    def greet(step, carry):
        peer = lax.rem(lat + lax.rem(step, 32), 32)
        column = 2 * x + lax.rem(half + step // 32, 2)
        pl.semaphore_signal(barrier, inc=1, device_id=(peer, column), device_id_type=MESH)
        return carry

    lax.fori_loop(1, 64, greet, 0)
    for step in range(1, 4):
        pl.semaphore_signal(
            barrier, inc=1, device_id=(lat, 2 * lax.rem(x + step, 4) + half), device_id_type=MESH
        )
    outer = jnp.where(half == 1, right, left)
    pl.semaphore_signal(barrier, inc=1, device_id=(lat, outer), device_id_type=MESH)

    load.wait()
    es[0] = g[2:6, 0:REACH, :]
    es[1] = g[2:6, SLAB - REACH : SLAB, :]
    lane_block = lax.broadcasted_iota(jnp.int32, (8, 128), 1) // 32

    def pack(strip, carry):
        at = pl.ds(pl.multiple_of(strip * 8, 8), 8)
        for tile in range(2):
            rows = [g[2 + a, at, tile * 128 : tile * 128 + 128] for a in range(4)]
            for q in range(4):
                made = rows[q] if q else rows[0]
                for a in range(4):
                    if a != q:
                        moved = pltpu.roll(rows[a], ((a - q) * 32) % 128, 1)
                        made = jnp.where(lane_block == a, moved, made)
                pk[tile * 4 + q, at, :] = made
        return carry

    lax.fori_loop(0, PAD // 8, pack, 0)

    pl.semaphore_wait(barrier, 63 + 3 + 1)

    sends = []
    for turn in range(2):
        chunk = lax.rem(half + 1 + turn, 2)
        for step in (2, 1, 3):
            there = lax.rem(x + step, 4)
            copy = pltpu.make_async_remote_copy(
                src_ref=pk.at[2 * there + chunk],
                dst_ref=xr.at[turn, x],
                send_sem=s1_send.at[turn, step - 1],
                recv_sem=s1_recv.at[turn, step - 1],
                device_id=(lat, 2 * there + half),
                device_id_type=MESH,
            )
            copy.start()
            sends.append(copy)
        if turn == 0:
            edges = []
            for side, there in ((1, left), (0, right)):
                copy = pltpu.make_async_remote_copy(
                    src_ref=es.at[1 - side],
                    dst_ref=e.at[side, pl.ds(2, 4)],
                    send_sem=h_send.at[side],
                    recv_sem=h_recv.at[side],
                    device_id=(lat, there),
                    device_id_type=MESH,
                )
                copy.start()
                edges.append(copy)
    for turn in range(2):
        chunk = lax.rem(half + 1 + turn, 2)
        xr[turn, x] = pk[2 * x + chunk]

    up, down = lax.rem(lat + 1, 32), lax.rem(lat + 31, 32)

    def row_copies(buffer, index, send, recv):
        return (
            pltpu.make_async_remote_copy(
                src_ref=buffer.at[index + (pl.ds(4, 2),)],
                dst_ref=buffer.at[index + (pl.ds(0, 2),)],
                send_sem=send.at[0], recv_sem=recv.at[0],
                device_id=(up, lon), device_id_type=MESH,
            ),
            pltpu.make_async_remote_copy(
                src_ref=buffer.at[index + (pl.ds(2, 2),)],
                dst_ref=buffer.at[index + (pl.ds(6, 2),)],
                send_sem=send.at[1], recv_sem=recv.at[1],
                device_id=(down, lon), device_id_type=MESH,
            ),
        )

    halo = [
        row_copies(g, (), c_send.at[0], c_recv.at[0]),
        row_copies(e, (0,), c_send.at[1], c_recv.at[1]),
        row_copies(e, (1,), c_send.at[2], c_recv.at[2]),
    ]

    def start_rows(pair):
        @pl.when(lat < 31)
        def _():
            pair[0].start()

        @pl.when(lat > 0)
        def _():
            pair[1].start()

    start_rows(halo[0])

    @pl.when(lat == 0)
    def _():
        g[0:2] = jnp.zeros((2, PAD, 256), F32)
        e[:, 0:2] = jnp.zeros((2, 2, REACH, 256), F32)

    @pl.when(lat == 31)
    def _():
        g[6:8] = jnp.zeros((2, PAD, 256), F32)
        e[:, 6:8] = jnp.zeros((2, 2, REACH, 256), F32)

    group = lax.broadcasted_iota(jnp.int32, (GW, 256), 1) // GW

    def spread(k, carry):
        high, low = split(weight[k])
        high, low = high.astype(F32), low.astype(F32)
        for at in range(8):
            rows = pl.ds(pl.multiple_of(k * 256 + at * GW, GW), GW)
            bdh[rows, :] = jnp.where(group == at, high, 0.0).astype(BF16)
            bdl[rows, :] = jnp.where(group == at, low, 0.0).astype(BF16)
        return carry

    lax.fori_loop(0, KERNELS, spread, 0)
    load_even.wait()
    load_odd.wait()

    def transform(turn):
        s0, s1, s2, s3 = (xr[turn, i] for i in range(4))
        p02, p13 = s0 + s2, s1 + s3
        for at, value in ((0, p02 + p13), (1, p02 - p13)):
            high, low = split(value)
            both = jnp.concatenate([high, low], axis=1)
            rows = pl.ds(at * 256, 256)
            first = jnp.dot(te[0, rows, :], both, preferred_element_type=F32)
            second = jnp.dot(te[1, rows, :], high, preferred_element_type=F32)
            total = first[:, :128] + first[:, 128:] + second
            sp[turn, :, at * 8 : at * 8 + 8, :] = total.reshape(32, 8, 128)
        high, low = split(jnp.concatenate([s0 - s2, s1 - s3], axis=0))
        both = jnp.concatenate([high, low], axis=1)
        first = jnp.dot(to[0], both, preferred_element_type=F32)
        second = jnp.dot(to[1], high, preferred_element_type=F32)
        total = first[:, :128] + first[:, 128:] + second
        sp[turn, :, 16:32, :] = total.reshape(32, 16, 128)

    mine = half * 32 + lat

    def scatter(turn):
        column = 2 * x + lax.rem(half + 1 + turn, 2)

        def send(step, carry):
            there = (
                lax.rem(z_lo + step // 8, 4) * 8
                + lax.rem(y + lax.rem(step, 8) // 2, 4) * 2
                + lax.rem(core + step, 2)
            )
            pltpu.make_async_remote_copy(
                src_ref=sp.at[turn, there],
                dst_ref=r.at[mine],
                send_sem=s3_send,
                recv_sem=s3_recv,
                device_id=(there, column),
                device_id_type=MESH,
            ).start()
            return carry

        lax.fori_loop(turn, 32, send, 0)

    for turn in range(2):
        for copy in sends[turn * 3 : turn * 3 + 3]:
            copy.wait_recv()
        transform(turn)
        if turn == 0:
            for copy in edges:
                copy.wait_recv()
            start_rows(halo[1])
            start_rows(halo[2])
        scatter(turn)
    own = pltpu.make_async_copy(sp.at[1, lat], r.at[mine], own_sem)
    own.start()

    @pl.when(lat > 0)
    def _():
        for pair in halo:
            pair[0].wait_recv()

    @pl.when(lat < 31)
    def _():
        for pair in halo:
            pair[1].wait_recv()

    for row in range(8):
        for h in range(2):
            lanes = slice(h * 128, h * 128 + 128)
            f[h, row, 0:REACH, :] = e[0, row, :, lanes]
            f[h, row, REACH : REACH + SLAB, :] = g[row, 0:SLAB, lanes]
            f[h, row, REACH + SLAB : 2 * REACH + SLAB, :] = e[1, row, :, lanes]
            f[h, row, 2 * REACH + SLAB : SPAN, :] = jnp.zeros((SPAN - 2 * REACH - SLAB, 128), F32)

    def row_conv(a, carry):
        def strip(at, inner):
            sums = [jnp.zeros((16, 256), F32) for _ in range(KERNELS)]
            for s in range(SLOTS):
                begin = at * 16 + REACH + shifts[a, s]
                taken = jnp.concatenate([f[h, a + s % 5, pl.ds(begin, 16), :] for h in range(2)], axis=1)
                for k in range(KERNELS):
                    sums[k] = sums[k] + psi[a, s * KERNELS + k] * taken
            rows = pl.ds(pl.multiple_of(at * 16, 16), 16)
            for k in range(KERNELS):
                high, low = split(sums[k])
                gh[rows, k * 256 : k * 256 + 256] = high
                gl[rows, k * 256 : k * 256 + 256] = low
            return inner

        lax.fori_loop(0, STRIPS, strip, 0)
        total = jnp.dot(gh[...], bdh[...], preferred_element_type=F32)
        total += jnp.dot(gl[...], bdh[...], preferred_element_type=F32)
        total += jnp.dot(gh[...], bdl[...], preferred_element_type=F32)
        conv[a] = total[:SLAB]
        return carry

    lax.fori_loop(0, 4, row_conv, 0)

    own.wait()
    everyone = r.at[pl.ds(0, 63)]
    pltpu.make_async_copy(everyone, everyone, s3_recv).wait()
    from_row = lax.broadcasted_iota(jnp.int32, (128, 128), 0)
    to_lane = lax.broadcasted_iota(jnp.int32, (128, 128), 1)
    lane_of = (from_row % 32) * 4 + from_row // 32
    reorder = jnp.where(to_lane == lane_of, 1.0, 0.0).astype(BF16)
    block = lax.broadcasted_iota(jnp.int32, (32, 128), 1) // 32
    for quad in range(8):
        parts = [r[0:32, quad * 4 + i, :] + r[32:64, quad * 4 + i, :] for i in range(4)]
        turned = jnp.concatenate(parts, axis=0).T
        rows = [turned[a * 32 : a * 32 + 32, :] for a in range(4)]
        made = []
        for i in range(4):
            one = rows[i]
            for a in range(4):
                if a != i:
                    one = jnp.where(block == a, pltpu.roll(rows[a], ((a - i) * 32) % 128, 1), one)
            made.append(one)
        high, low = split(jnp.concatenate(made, axis=0))
        high = jnp.dot(high, reorder, preferred_element_type=F32).astype(BF16)
        low = jnp.dot(low, reorder, preferred_element_type=F32).astype(BF16)
        for n in range(2):
            order = ORDER_OF[quad * 2 + n]
            lhs[order, 0:64, :] = high[n * 64 : n * 64 + 64]
            lhs[order, 64:128, :] = low[n * 64 : n * 64 + 64]

    for copy in sends:
        copy.wait_send()
    for copy in edges:
        copy.wait_send()

    @pl.when(lat < 31)
    def _():
        for pair in halo:
            pair[0].wait_send()

    @pl.when(lat > 0)
    def _():
        for pair in halo:
            pair[1].wait_send()

    pltpu.make_async_copy(everyone, everyone, s3_send).wait()


def legendre_kernel(lhs, legendre, out):
    high, low = split(legendre[0])
    right = jnp.concatenate([high, low], axis=1)
    top, bottom = lhs[0, 0:64, :], lhs[0, 64:128, :]
    left = jnp.concatenate(
        [
            jnp.concatenate([top, top], axis=1),
            jnp.concatenate([bottom, jnp.zeros_like(bottom)], axis=1),
        ],
        axis=0,
    )
    both = lax.dot_general(left, right, (((1,), (1,)), ((), ())), preferred_element_type=F32)
    out[0] = both[0:64] + both[64:128]


def shards(field, legendre, shifts, psi, kernel_weight):
    even, odd = fourier_tables()
    padded = jnp.pad(field, ((0, 0), (0, PAD - SLAB), (0, 0)))
    vmem = pl.BlockSpec(memory_space=pltpu.VMEM)
    smem = pl.BlockSpec(memory_space=pltpu.SMEM)
    hbm = pl.BlockSpec(memory_space=pl.ANY)
    dma = pltpu.SemaphoreType.DMA
    conv, lhs = pl.pallas_call(
        main_kernel,
        out_shape=(
            jax.ShapeDtypeStruct((4, SLAB, 256), F32),
            jax.ShapeDtypeStruct((16, 128, 128), BF16),
        ),
        in_specs=[smem, smem, hbm, vmem, hbm, hbm],
        out_specs=(vmem, vmem),
        scratch_shapes=[
            pltpu.VMEM((8, PAD, 256), F32),
            pltpu.VMEM((2, 8, REACH, 256), F32),
            pltpu.VMEM((2, 8, SPAN, 128), F32),
            pltpu.VMEM((8, PAD, 128), F32),
            pltpu.VMEM((2, 4, PAD, 128), F32),
            pltpu.VMEM((2, 32, 32, 128), F32),
            pltpu.VMEM((64, 32, 128), F32),
            pltpu.VMEM((16 * STRIPS, KERNELS * 256), BF16),
            pltpu.VMEM((16 * STRIPS, KERNELS * 256), BF16),
            pltpu.VMEM((KERNELS * 256, 256), BF16),
            pltpu.VMEM((KERNELS * 256, 256), BF16),
            pltpu.VMEM((2, 512, PAD), BF16),
            pltpu.VMEM((2, 512, 2 * PAD), BF16),
            pltpu.VMEM((2, 4, REACH, 256), F32),
            dma,
            dma((2,)),
            dma((2, 3)),
            dma((2, 3)),
            dma((2,)),
            dma((2,)),
            dma((3, 2)),
            dma((3, 2)),
            dma,
            dma,
            dma,
        ],
        compiler_params=pltpu.CompilerParams(
            collective_id=0, has_side_effects=True, vmem_limit_bytes=40 * 1024 * 1024
        ),
        cost_estimate=pl.CostEstimate(flops=4_000_000_000, bytes_accessed=8_000_000, transcendentals=0),
        name="spectrum_and_convolution",
    )(shifts, psi.reshape(4, SLOTS * KERNELS), padded, kernel_weight, jnp.asarray(even), jnp.asarray(odd))
    coefficients = pl.pallas_call(
        legendre_kernel,
        grid=(16,),
        out_shape=jax.ShapeDtypeStruct((16, 64, 720), F32),
        in_specs=[
            pl.BlockSpec((1, 128, 128), lambda m: (m, 0, 0)),
            pl.BlockSpec((1, 720, 128), lambda m: (m, 0, 0)),
        ],
        out_specs=pl.BlockSpec((1, 64, 720), lambda m: (m, 0, 0)),
        compiler_params=pltpu.CompilerParams(vmem_limit_bytes=16 * 1024 * 1024),
        cost_estimate=pl.CostEstimate(flops=800_000_000, bytes_accessed=10_000_000, transcendentals=0),
        name="legendre",
    )(lhs, legendre)
    coefficients = coefficients.reshape(16, 2, GW, 720).transpose(0, 3, 1, 2)
    return coefficients, conv


def solution(mesh):
    placed = (
        P("lat", "lon", None),
        P("lat", None, None),
        P("lat", None),
        P("lat", None, None),
        P(),
    )
    return jax.shard_map(
        shards,
        mesh=mesh,
        in_specs=placed,
        out_specs=(P("lat", None, None, "lon"), P("lat", "lon", None)),
        check_vma=False,
    )
```

```python
import jax
import jax.numpy as jnp
import ml_dtypes
import numpy as np
from jax import lax
from jax.experimental import pallas as pl
from jax.experimental.pallas import tpu as pltpu
from jax.sharding import PartitionSpec as P

LON = 1440
ORDERS = 512
SLAB = 180
PAD = 184
GW = 32
KERNELS = 9
SLOTS = 20
RADIUS = 2
REACH = 16
STRIPS = 12
SPAN = 232
MESH = pl.DeviceIdType.MESH
F32 = jnp.float32
BF16 = jnp.bfloat16
ORDER_OF = [0, 4, 8, 12, 2, 6, 10, 14, 1, 3, 5, 7, 9, 11, 13, 15]


def two_parts(table):
    table = np.asarray(table, np.float32)
    high = table.astype(ml_dtypes.bfloat16)
    low = (table - high.astype(np.float32)).astype(ml_dtypes.bfloat16)
    return np.stack([high, low])


def fourier_tables():
    even, odd = [], []
    for half in range(2):
        j = SLAB * half + np.arange(PAD)
        live = (np.arange(PAD) < SLAB).astype(np.float64)

        def rows(orders, lead):
            turn = (np.asarray(orders)[:, None] * (j[None, :] + lead)) % LON
            angle = turn * (2.0 * np.pi / LON)
            both = np.stack([np.cos(angle), -np.sin(angle)], axis=1) * live
            return both.reshape(-1, PAD)

        owner = np.arange(32)[:, None] * 16
        zero = (owner + np.arange(0, 16, 4)).reshape(-1)
        two = (owner + np.arange(2, 16, 4)).reshape(-1)
        ones = (owner + np.arange(1, 16, 2)).reshape(-1)
        even.append(two_parts(np.concatenate([rows(zero, 0), rows(two, 0)])))
        odd.append(two_parts(np.concatenate([rows(ones, 0), rows(ones, 360)], axis=1)))
    return np.stack(even), np.stack(odd)


def split(value):
    high = value.astype(BF16)
    return high, (value - high.astype(F32)).astype(BF16)


def main_kernel(
    shifts_in, psi_in, field, weight_in, even, odd, legendre,
    conv, lhs, lp,
    g, gh_rows, e, f, pk, xr, sp, r, gh, gl, bdh, bdl, te, to, es, weight, lf, turned_l, shifts, psi,
    load_sem, table_sem, s1_send, s1_recv, h_send, h_recv, c_send, c_recv, s3_send, s3_recv, own_sem,
):
    lat = lax.axis_index("lat")
    lon = lax.axis_index("lon")
    x, half = lon // 2, lon % 2
    z_lo, y, core = lat // 8, (lat // 2) % 4, lat % 2
    right = lax.rem(lon + 1, 8)
    left = lax.rem(lon + 7, 8)

    loads = [
        pltpu.make_async_copy(field.at[:, a, :], g.at[a], load_sem.at[a])
        for a in range(4)
    ]
    tables = [
        pltpu.make_async_copy(weight_in, weight, table_sem.at[0]),
        pltpu.make_async_copy(even.at[half], te, table_sem.at[1]),
        pltpu.make_async_copy(odd.at[half], to, table_sem.at[2]),
        pltpu.make_async_copy(psi_in, psi, table_sem.at[3]),
        pltpu.make_async_copy(shifts_in, shifts, table_sem.at[4]),
        pltpu.make_async_copy(legendre, lf, table_sem.at[5]),
    ]
    for copy in loads + tables:
        copy.start()
    pk[:, SLAB:PAD, :] = jnp.zeros((8, PAD - SLAB, 128), F32)

    barrier = pltpu.get_barrier_semaphore()

    def greet(step, carry):
        peer = lax.rem(lat + lax.rem(step, 32), 32)
        column = 2 * x + lax.rem(half + step // 32, 2)
        pl.semaphore_signal(barrier, inc=1, device_id=(peer, column), device_id_type=MESH)
        return carry

    lax.fori_loop(1, 64, greet, 0)
    for step in range(1, 4):
        pl.semaphore_signal(
            barrier, inc=1, device_id=(lat, 2 * lax.rem(x + step, 4) + half), device_id_type=MESH
        )
    outer = jnp.where(half == 1, right, left)
    pl.semaphore_signal(barrier, inc=1, device_id=(lat, outer), device_id_type=MESH)

    for copy in loads:
        copy.wait()
    es[0] = g[:, 0:REACH, :]
    es[1] = g[:, SLAB - REACH : SLAB, :]
    def pack(at, count):
        lane_block = lax.broadcasted_iota(jnp.int32, (count, 128), 1) // 32
        for tile in range(2):
            rows = [g[a, at, tile * 128 : tile * 128 + 128] for a in range(4)]
            for q in range(4):
                made = rows[q]
                for a in range(4):
                    if a != q:
                        moved = pltpu.roll(rows[a], ((a - q) * 32) % 128, 1)
                        made = jnp.where(lane_block == a, moved, made)
                pk[tile * 4 + q, at, :] = made

    def pack_strip(strip, carry):
        pack(pl.ds(pl.multiple_of(strip * 8, 8), 8), 8)
        return carry

    lax.fori_loop(0, SLAB // 8, pack_strip, 0)
    pack(pl.ds(SLAB - 4, 4), 4)

    pl.semaphore_wait(barrier, 63 + 3 + 1)

    sends = []
    for turn in range(2):
        chunk = lax.rem(half + 1 + turn, 2)
        for step in (2, 1, 3):
            there = lax.rem(x + step, 4)
            copy = pltpu.make_async_remote_copy(
                src_ref=pk.at[2 * there + chunk],
                dst_ref=xr.at[turn, x],
                send_sem=s1_send.at[turn, step - 1],
                recv_sem=s1_recv.at[turn, step - 1],
                device_id=(lat, 2 * there + half),
                device_id_type=MESH,
            )
            copy.start()
            sends.append(copy)
        if turn == 0:
            edges = []
            for side, there in ((1, left), (0, right)):
                copy = pltpu.make_async_remote_copy(
                    src_ref=es.at[1 - side],
                    dst_ref=e.at[side, pl.ds(2, 4)],
                    send_sem=h_send.at[side],
                    recv_sem=h_recv.at[side],
                    device_id=(lat, there),
                    device_id_type=MESH,
                )
                copy.start()
                edges.append(copy)
    for turn in range(2):
        chunk = lax.rem(half + 1 + turn, 2)
        xr[turn, x] = pk[2 * x + chunk]

    up, down = lax.rem(lat + 1, 32), lax.rem(lat + 31, 32)

    def row_copies(rows, above, below, send, recv):
        return (
            pltpu.make_async_remote_copy(
                src_ref=rows.at[pl.ds(2, 2)], dst_ref=above,
                send_sem=send.at[0], recv_sem=recv.at[0],
                device_id=(up, lon), device_id_type=MESH,
            ),
            pltpu.make_async_remote_copy(
                src_ref=rows.at[pl.ds(0, 2)], dst_ref=below,
                send_sem=send.at[1], recv_sem=recv.at[1],
                device_id=(down, lon), device_id_type=MESH,
            ),
        )

    halo = [row_copies(g, gh_rows.at[0], gh_rows.at[1], c_send.at[0], c_recv.at[0])] + [
        row_copies(
            e.at[side, pl.ds(2, 4)], e.at[side, pl.ds(0, 2)], e.at[side, pl.ds(6, 2)],
            c_send.at[1 + side], c_recv.at[1 + side],
        )
        for side in range(2)
    ]

    def start_rows(pair):
        @pl.when(lat < 31)
        def _():
            pair[0].start()

        @pl.when(lat > 0)
        def _():
            pair[1].start()

    start_rows(halo[0])

    @pl.when(lat == 0)
    def _():
        gh_rows[0] = jnp.zeros((2, SLAB, 256), F32)
        e[:, 0:2] = jnp.zeros((2, 2, REACH, 256), F32)

    @pl.when(lat == 31)
    def _():
        gh_rows[1] = jnp.zeros((2, SLAB, 256), F32)
        e[:, 6:8] = jnp.zeros((2, 2, REACH, 256), F32)

    tables[0].wait()
    group = lax.broadcasted_iota(jnp.int32, (GW, 256), 1) // GW

    def spread(k, carry):
        high, low = split(weight[k])
        high, low = high.astype(F32), low.astype(F32)
        for at in range(8):
            rows = pl.ds(pl.multiple_of(k * 256 + at * GW, GW), GW)
            bdh[rows, :] = jnp.where(group == at, high, 0.0).astype(BF16)
            bdl[rows, :] = jnp.where(group == at, low, 0.0).astype(BF16)
        return carry

    lax.fori_loop(0, KERNELS, spread, 0)
    tables[1].wait()
    tables[2].wait()

    def transform(turn):
        s0, s1, s2, s3 = (xr[turn, i] for i in range(4))
        p02, p13 = s0 + s2, s1 + s3
        for at, value in ((0, p02 + p13), (1, p02 - p13)):
            high, low = split(value)
            both = jnp.concatenate([high, low], axis=1)
            rows = pl.ds(at * 256, 256)
            first = jnp.dot(te[0, rows, :], both, preferred_element_type=F32)
            second = jnp.dot(te[1, rows, :], high, preferred_element_type=F32)
            total = first[:, :128] + first[:, 128:] + second
            sp[turn, :, at * 8 : at * 8 + 8, :] = total.reshape(32, 8, 128)
        high, low = split(jnp.concatenate([s0 - s2, s1 - s3], axis=0))
        both = jnp.concatenate([high, low], axis=1)
        first = jnp.dot(to[0], both, preferred_element_type=F32)
        second = jnp.dot(to[1], high, preferred_element_type=F32)
        total = first[:, :128] + first[:, 128:] + second
        sp[turn, :, 16:32, :] = total.reshape(32, 16, 128)

    mine = half * 32 + lat

    def scatter(turn):
        column = 2 * x + lax.rem(half + 1 + turn, 2)

        def send(step, carry):
            there = (
                lax.rem(z_lo + step // 8, 4) * 8
                + lax.rem(y + lax.rem(step, 8) // 2, 4) * 2
                + lax.rem(core + step, 2)
            )
            pltpu.make_async_remote_copy(
                src_ref=sp.at[turn, there],
                dst_ref=r.at[mine],
                send_sem=s3_send,
                recv_sem=s3_recv,
                device_id=(there, column),
                device_id_type=MESH,
            ).start()
            return carry

        lax.fori_loop(turn, 32, send, 0)

    for turn in range(2):
        for copy in sends[turn * 3 : turn * 3 + 3]:
            copy.wait_recv()
        transform(turn)
        if turn == 0:
            for copy in edges:
                copy.wait_recv()
            start_rows(halo[1])
            start_rows(halo[2])
        scatter(turn)
    own = pltpu.make_async_copy(sp.at[1, lat], r.at[mine], own_sem)
    own.start()

    tables[5].wait()

    def prepare(m, carry):
        for block in range(6):
            count = min(128, 720 - block * 128)
            columns = slice(block * 128, block * 128 + count)
            turned_l[block, :, 0:count] = lf[m, columns, :].T
            for a in range(4):
                high, low = split(turned_l[block, pl.ds(a, 32, stride=4), :])
                lp[m, a * 32 : a * 32 + 32, columns] = high[:, :count]
                lp[m, 128 + a * 32 : 160 + a * 32, columns] = low[:, :count]
        return carry

    lax.fori_loop(0, 16, prepare, 0)

    @pl.when(lat > 0)
    def _():
        for pair in halo:
            pair[0].wait_recv()

    @pl.when(lat < 31)
    def _():
        for pair in halo:
            pair[1].wait_recv()

    for row in range(8):
        source = g.at[row - 2] if 2 <= row < 6 else gh_rows.at[row // 6, row % 2]
        for h in range(2):
            lanes = slice(h * 128, h * 128 + 128)
            f[h, row, 0:REACH, :] = e[0, row, :, lanes]
            f[h, row, REACH : REACH + SLAB, :] = source[:, lanes]
            f[h, row, REACH + SLAB : 2 * REACH + SLAB, :] = e[1, row, :, lanes]
            f[h, row, 2 * REACH + SLAB : SPAN, :] = jnp.zeros((SPAN - 2 * REACH - SLAB, 128), F32)

    tables[3].wait()
    tables[4].wait()

    def row_conv(a, carry):
        def strip(at, inner):
            sums = [jnp.zeros((16, 256), F32) for _ in range(KERNELS)]
            for s in range(SLOTS):
                begin = at * 16 + REACH + shifts[a, s]
                taken = jnp.concatenate([f[h, a + s % 5, pl.ds(begin, 16), :] for h in range(2)], axis=1)
                for k in range(KERNELS):
                    sums[k] = sums[k] + psi[k, a, s] * taken
            rows = pl.ds(pl.multiple_of(at * 16, 16), 16)
            for k in range(KERNELS):
                high, low = split(sums[k])
                gh[rows, k * 256 : k * 256 + 256] = high
                gl[rows, k * 256 : k * 256 + 256] = low
            return inner

        lax.fori_loop(0, STRIPS, strip, 0)
        total = jnp.dot(gh[...], bdh[...], preferred_element_type=F32)
        total += jnp.dot(gl[...], bdh[...], preferred_element_type=F32)
        total += jnp.dot(gh[...], bdl[...], preferred_element_type=F32)
        conv[a] = total[:SLAB]
        return carry

    lax.fori_loop(0, 4, row_conv, 0)

    own.wait()
    everyone = r.at[pl.ds(0, 63)]
    pltpu.make_async_copy(everyone, everyone, s3_recv).wait()
    block = lax.broadcasted_iota(jnp.int32, (32, 128), 1) // 32
    for quad in range(8):
        parts = [r[0:32, quad * 4 + i, :] + r[32:64, quad * 4 + i, :] for i in range(4)]
        turned = jnp.concatenate(parts, axis=0).T
        rows = [turned[a * 32 : a * 32 + 32, :] for a in range(4)]
        made = []
        for i in range(4):
            one = rows[i]
            for a in range(4):
                if a != i:
                    one = jnp.where(block == a, pltpu.roll(rows[a], ((a - i) * 32) % 128, 1), one)
            made.append(one)
        high, low = split(jnp.concatenate(made, axis=0))
        for n in range(2):
            order = ORDER_OF[quad * 2 + n]
            lhs[order, 0:64, :] = high[n * 64 : n * 64 + 64]
            lhs[order, 64:128, :] = low[n * 64 : n * 64 + 64]

    for copy in sends:
        copy.wait_send()
    for copy in edges:
        copy.wait_send()

    @pl.when(lat < 31)
    def _():
        for pair in halo:
            pair[0].wait_send()

    @pl.when(lat > 0)
    def _():
        for pair in halo:
            pair[1].wait_send()

    pltpu.make_async_copy(everyone, everyone, s3_send).wait()


def legendre_kernel(lhs, lp, conv, out, moved, made, out_sem, move_sem):
    moves = [pltpu.make_async_copy(conv.at[a], moved.at[:, a, :], move_sem.at[a]) for a in range(4)]
    for copy in moves:
        copy.start()

    def leaving(m):
        return pltpu.make_async_copy(made.at[m], out.at[m], out_sem.at[m])

    def order(m, carry):
        top, bottom = lhs[m, 0:64, :], lhs[m, 64:128, :]
        left = jnp.concatenate(
            [
                jnp.concatenate([top, top], axis=1),
                jnp.concatenate([bottom, jnp.zeros_like(bottom)], axis=1),
            ],
            axis=0,
        )
        both = jnp.dot(left, lp[m], preferred_element_type=F32)
        made[m] = both[0:64] + both[64:128]
        leaving(m).start()
        return carry

    lax.fori_loop(0, 16, order, 0, unroll=4)
    for copy in moves:
        copy.wait()
    lax.fori_loop(0, 16, lambda m, carry: leaving(m).wait(), None)


def shards(field, legendre, shifts, psi, kernel_weight):
    even, odd = fourier_tables()
    vmem = pl.BlockSpec(memory_space=pltpu.VMEM)
    hbm = pl.BlockSpec(memory_space=pltpu.HBM)
    dma = pltpu.SemaphoreType.DMA
    conv, lhs, prepared = pl.pallas_call(
        main_kernel,
        out_shape=(
            pltpu.VMEM((4, SLAB, 256), F32),
            pltpu.VMEM((16, 128, 128), BF16),
            pltpu.VMEM((16, 256, 720), BF16),
        ),
        in_specs=[hbm] * 7,
        out_specs=(vmem, vmem, vmem),
        scratch_shapes=[
            pltpu.VMEM((4, SLAB, 256), F32),
            pltpu.VMEM((2, 2, SLAB, 256), F32),
            pltpu.VMEM((2, 8, REACH, 256), F32),
            pltpu.VMEM((2, 8, SPAN, 128), F32),
            pltpu.VMEM((8, PAD, 128), F32),
            pltpu.VMEM((2, 4, PAD, 128), F32),
            pltpu.VMEM((2, 32, 32, 128), F32),
            pltpu.VMEM((64, 32, 128), F32),
            pltpu.VMEM((16 * STRIPS, KERNELS * 256), BF16),
            pltpu.VMEM((16 * STRIPS, KERNELS * 256), BF16),
            pltpu.VMEM((KERNELS * 256, 256), BF16),
            pltpu.VMEM((KERNELS * 256, 256), BF16),
            pltpu.VMEM((2, 512, PAD), BF16),
            pltpu.VMEM((2, 512, 2 * PAD), BF16),
            pltpu.VMEM((2, 4, REACH, 256), F32),
            pltpu.VMEM((KERNELS, GW, 256), F32),
            pltpu.VMEM((16, 720, 128), F32),
            pltpu.VMEM((6, 128, 128), F32),
            pltpu.SMEM((4, SLOTS), jnp.int32),
            pltpu.SMEM((KERNELS, 4, SLOTS), F32),
            dma((4,)),
            dma((6,)),
            dma((2, 3)),
            dma((2, 3)),
            dma((2,)),
            dma((2,)),
            dma((3, 2)),
            dma((3, 2)),
            dma,
            dma,
            dma,
        ],
        compiler_params=pltpu.CompilerParams(
            collective_id=0, has_side_effects=True, vmem_limit_bytes=44 * 1024 * 1024
        ),
        cost_estimate=pl.CostEstimate(flops=4_000_000_000, bytes_accessed=8_000_000, transcendentals=0),
        name="spectrum_and_convolution",
    )(
        *(
            pltpu.with_memory_space_constraint(value, pltpu.HBM)
            for value in (
                shifts,
                psi.transpose(2, 0, 1),
                field.transpose(1, 0, 2),
                kernel_weight,
                jnp.asarray(even),
                jnp.asarray(odd),
                legendre,
            )
        )
    )
    coefficients, moved = pl.pallas_call(
        legendre_kernel,
        out_shape=(
            jax.ShapeDtypeStruct((16, 64, 720), F32),
            jax.ShapeDtypeStruct((SLAB, 4, 256), F32),
        ),
        in_specs=[vmem, vmem, vmem],
        out_specs=(hbm, hbm),
        scratch_shapes=[pltpu.VMEM((16, 64, 720), F32), dma((16,)), dma((4,))],
        compiler_params=pltpu.CompilerParams(vmem_limit_bytes=24 * 1024 * 1024),
        cost_estimate=pl.CostEstimate(flops=800_000_000, bytes_accessed=10_000_000, transcendentals=0),
        name="legendre",
    )(lhs, prepared, conv)
    coefficients = coefficients.reshape(16, 2, GW, 720).transpose(0, 3, 1, 2)
    return coefficients, moved.transpose(1, 0, 2)


def solution(mesh):
    placed = (
        P("lat", "lon", None),
        P("lat", None, None),
        P("lat", None),
        P("lat", None, None),
        P(),
    )
    return jax.shard_map(
        shards,
        mesh=mesh,
        in_specs=placed,
        out_specs=(P("lat", None, None, "lon"), P("lat", "lon", None)),
        check_vma=False,
    )
```

```python
import jax
import jax.numpy as jnp
import ml_dtypes
import numpy as np
from jax import lax
from jax.experimental import pallas as pl
from jax.experimental.pallas import tpu as pltpu
from jax.sharding import PartitionSpec as P

LON = 1440
ORDERS = 512
SLAB = 180
PAD = 184
GW = 32
KERNELS = 9
SLOTS = 20
RADIUS = 2
REACH = 16
STRIDE = 2 * RADIUS + 1
ROWS = 192
SPAN = 232
MESH = pl.DeviceIdType.MESH
F32 = jnp.float32
BF16 = jnp.bfloat16
ORDER_OF = [0, 4, 8, 12, 2, 6, 10, 14, 1, 3, 5, 7, 9, 11, 13, 15]


def two_parts(table):
    table = np.asarray(table, np.float32)
    high = table.astype(ml_dtypes.bfloat16)
    low = (table - high.astype(np.float32)).astype(ml_dtypes.bfloat16)
    return np.stack([high, low])


def fourier_tables():
    even, odd = [], []
    for half in range(2):
        j = SLAB * half + np.arange(PAD)
        live = (np.arange(PAD) < SLAB).astype(np.float64)

        def rows(orders, lead):
            turn = (np.asarray(orders)[:, None] * (j[None, :] + lead)) % LON
            angle = turn * (2.0 * np.pi / LON)
            both = np.stack([np.cos(angle), -np.sin(angle)], axis=1) * live
            return both.reshape(-1, PAD)

        owner = np.arange(32)[:, None] * 16
        zero = (owner + np.arange(0, 16, 4)).reshape(-1)
        two = (owner + np.arange(2, 16, 4)).reshape(-1)
        ones = (owner + np.arange(1, 16, 2)).reshape(-1)
        even.append(two_parts(np.concatenate([rows(zero, 0), rows(two, 0)])))
        odd.append(two_parts(np.concatenate([rows(ones, 0), rows(ones, 360)], axis=1)))
    return np.stack(even), np.stack(odd)


def split(value):
    high = value.astype(BF16)
    return high, (value - high.astype(F32)).astype(BF16)


def main_kernel(
    shifts_in, psi_in, field, weight_in, even, odd, legendre,
    conv, lhs, lp,
    g, gh_rows, e, f, pk, xr, sp, r, taps_a, taps_b, mix_a, mix_b, te, to, es, weight, lf, turned_l, shifts, psi,
    load_sem, table_sem, s1_send, s1_recv, h_send, h_recv, c_send, c_recv, s3_send, s3_recv, own_sem,
):
    lat = lax.axis_index("lat")
    lon = lax.axis_index("lon")
    x, half = lon // 2, lon % 2
    z_lo, y, core = lat // 8, (lat // 2) % 4, lat % 2
    right = lax.rem(lon + 1, 8)
    left = lax.rem(lon + 7, 8)

    loads = [
        pltpu.make_async_copy(field.at[:, a, :], g.at[a], load_sem.at[a])
        for a in range(4)
    ]
    tables = [
        pltpu.make_async_copy(weight_in, weight, table_sem.at[0]),
        pltpu.make_async_copy(even.at[half], te, table_sem.at[1]),
        pltpu.make_async_copy(odd.at[half], to, table_sem.at[2]),
        pltpu.make_async_copy(psi_in, psi, table_sem.at[3]),
        pltpu.make_async_copy(shifts_in, shifts, table_sem.at[4]),
        pltpu.make_async_copy(legendre, lf, table_sem.at[5]),
    ]
    for copy in loads + tables:
        copy.start()
    pk[:, SLAB:PAD, :] = jnp.zeros((8, PAD - SLAB, 128), F32)

    barrier = pltpu.get_barrier_semaphore()

    def greet(step, carry):
        peer = lax.rem(lat + lax.rem(step, 32), 32)
        column = 2 * x + lax.rem(half + step // 32, 2)
        pl.semaphore_signal(barrier, inc=1, device_id=(peer, column), device_id_type=MESH)
        return carry

    lax.fori_loop(1, 64, greet, 0)
    for step in range(1, 4):
        pl.semaphore_signal(
            barrier, inc=1, device_id=(lat, 2 * lax.rem(x + step, 4) + half), device_id_type=MESH
        )
    outer = jnp.where(half == 1, right, left)
    pl.semaphore_signal(barrier, inc=1, device_id=(lat, outer), device_id_type=MESH)

    for copy in loads:
        copy.wait()
    es[0] = g[:, 0:REACH, :]
    es[1] = g[:, SLAB - REACH : SLAB, :]
    def pack(at, count):
        lane_block = lax.broadcasted_iota(jnp.int32, (count, 128), 1) // 32
        for tile in range(2):
            rows = [g[a, at, tile * 128 : tile * 128 + 128] for a in range(4)]
            for q in range(4):
                made = rows[q]
                for a in range(4):
                    if a != q:
                        moved = pltpu.roll(rows[a], ((a - q) * 32) % 128, 1)
                        made = jnp.where(lane_block == a, moved, made)
                pk[tile * 4 + q, at, :] = made

    def pack_strip(strip, carry):
        pack(pl.ds(pl.multiple_of(strip * 8, 8), 8), 8)
        return carry

    lax.fori_loop(0, SLAB // 8, pack_strip, 0)
    pack(pl.ds(SLAB - 4, 4), 4)

    pl.semaphore_wait(barrier, 63 + 3 + 1)

    sends = []
    for turn in range(2):
        chunk = lax.rem(half + 1 + turn, 2)
        for step in (2, 1, 3):
            there = lax.rem(x + step, 4)
            copy = pltpu.make_async_remote_copy(
                src_ref=pk.at[2 * there + chunk],
                dst_ref=xr.at[turn, x],
                send_sem=s1_send.at[turn, step - 1],
                recv_sem=s1_recv.at[turn, step - 1],
                device_id=(lat, 2 * there + half),
                device_id_type=MESH,
            )
            copy.start()
            sends.append(copy)
        if turn == 0:
            edges = []
            for side, there in ((1, left), (0, right)):
                copy = pltpu.make_async_remote_copy(
                    src_ref=es.at[1 - side],
                    dst_ref=e.at[side, pl.ds(2, 4)],
                    send_sem=h_send.at[side],
                    recv_sem=h_recv.at[side],
                    device_id=(lat, there),
                    device_id_type=MESH,
                )
                copy.start()
                edges.append(copy)
    for turn in range(2):
        chunk = lax.rem(half + 1 + turn, 2)
        xr[turn, x] = pk[2 * x + chunk]

    up, down = lax.rem(lat + 1, 32), lax.rem(lat + 31, 32)

    def row_copies(rows, above, below, send, recv):
        return (
            pltpu.make_async_remote_copy(
                src_ref=rows.at[pl.ds(2, 2)], dst_ref=above,
                send_sem=send.at[0], recv_sem=recv.at[0],
                device_id=(up, lon), device_id_type=MESH,
            ),
            pltpu.make_async_remote_copy(
                src_ref=rows.at[pl.ds(0, 2)], dst_ref=below,
                send_sem=send.at[1], recv_sem=recv.at[1],
                device_id=(down, lon), device_id_type=MESH,
            ),
        )

    halo = [row_copies(g, gh_rows.at[0], gh_rows.at[1], c_send.at[0], c_recv.at[0])] + [
        row_copies(
            e.at[side, pl.ds(2, 4)], e.at[side, pl.ds(0, 2)], e.at[side, pl.ds(6, 2)],
            c_send.at[1 + side], c_recv.at[1 + side],
        )
        for side in range(2)
    ]

    def start_rows(pair):
        @pl.when(lat < 31)
        def _():
            pair[0].start()

        @pl.when(lat > 0)
        def _():
            pair[1].start()

    start_rows(halo[0])

    @pl.when(lat == 0)
    def _():
        gh_rows[0] = jnp.zeros((2, SLAB, 256), F32)
        e[:, 0:2] = jnp.zeros((2, 2, REACH, 256), F32)

    @pl.when(lat == 31)
    def _():
        gh_rows[1] = jnp.zeros((2, SLAB, 256), F32)
        e[:, 6:8] = jnp.zeros((2, 2, REACH, 256), F32)

    mix_a[...] = jnp.zeros(mix_a.shape, BF16)
    mix_b[...] = jnp.zeros(mix_b.shape, BF16)
    tables[5].wait()

    def prepare(m, carry):
        for block in range(6):
            count = min(128, 720 - block * 128)
            columns = slice(block * 128, block * 128 + count)
            turned_l[block, :, 0:count] = lf[m, columns, :].T
            for a in range(4):
                high, low = split(turned_l[block, pl.ds(a, 32, stride=4), :])
                lp[m, a * 32 : a * 32 + 32, columns] = high[:, :count]
                lp[m, 128 + a * 32 : 160 + a * 32, columns] = low[:, :count]
        return carry

    lax.fori_loop(0, 16, prepare, 0, unroll=2)

    tables[1].wait()
    tables[2].wait()

    def transform(turn):
        s0, s1, s2, s3 = (xr[turn, i] for i in range(4))
        p02, p13 = s0 + s2, s1 + s3
        for at, value in ((0, p02 + p13), (1, p02 - p13)):
            high, low = split(value)
            both = jnp.concatenate([high, low], axis=1)
            rows = pl.ds(at * 256, 256)
            first = jnp.dot(te[0, rows, :], both, preferred_element_type=F32)
            second = jnp.dot(te[1, rows, :], high, preferred_element_type=F32)
            total = first[:, :128] + first[:, 128:] + second
            sp[turn, :, at * 8 : at * 8 + 8, :] = total.reshape(32, 8, 128)
        high, low = split(jnp.concatenate([s0 - s2, s1 - s3], axis=0))
        both = jnp.concatenate([high, low], axis=1)
        first = jnp.dot(to[0], both, preferred_element_type=F32)
        second = jnp.dot(to[1], high, preferred_element_type=F32)
        total = first[:, :128] + first[:, 128:] + second
        sp[turn, :, 16:32, :] = total.reshape(32, 16, 128)

    mine = half * 32 + lat

    def scatter(turn):
        column = 2 * x + lax.rem(half + 1 + turn, 2)

        def send(step, carry):
            there = (
                lax.rem(z_lo + lax.rem(step, 4), 4) * 8
                + lax.rem(y + lax.rem(step, 32) // 8, 4) * 2
                + lax.rem(core + step // 4, 2)
            )
            pltpu.make_async_remote_copy(
                src_ref=sp.at[turn, there],
                dst_ref=r.at[mine],
                send_sem=s3_send,
                recv_sem=s3_recv,
                device_id=(there, column),
                device_id_type=MESH,
            ).start()
            return carry

        lax.fori_loop(turn, 32, send, 0)

    for turn in range(2):
        for copy in sends[turn * 3 : turn * 3 + 3]:
            copy.wait_recv()
        transform(turn)
        if turn == 0:
            for copy in edges:
                copy.wait_recv()
            start_rows(halo[1])
            start_rows(halo[2])
        scatter(turn)
    own = pltpu.make_async_copy(sp.at[1, lat], r.at[mine], own_sem)
    own.start()

    @pl.when(lat > 0)
    def _():
        for pair in halo:
            pair[0].wait_recv()

    @pl.when(lat < 31)
    def _():
        for pair in halo:
            pair[1].wait_recv()

    def place(row, h, at, value):
        high = value.astype(BF16).astype(F32)
        f[0, h, row, at : at + value.shape[0], :] = high
        f[1, h, row, at : at + value.shape[0], :] = value - high

    for row in range(8):
        source = g.at[row - 2] if 2 <= row < 6 else gh_rows.at[row // 6, row % 2]
        for h in range(2):
            lanes = slice(h * 128, h * 128 + 128)
            place(row, h, 0, e[0, row, :, lanes])
            place(row, h, REACH, source[:, lanes])
            place(row, h, REACH + SLAB, e[1, row, :, lanes])
            f[:, h, row, 2 * REACH + SLAB : SPAN, :] = jnp.zeros((2, SPAN - 2 * REACH - SLAB, 128), F32)

    for table in (tables[0], tables[3], tables[4]):
        table.wait()
    group = lax.broadcasted_iota(jnp.int32, (GW, 128), 1) // GW

    def fill(a, quarter, taps, mix):
        for d in range(STRIDE):
            s = quarter * STRIDE + d
            mixed = psi[0, a, s] * weight[0]
            for k in range(1, KERNELS):
                mixed = mixed + psi[k, a, s] * weight[k]
            high = mixed.astype(BF16).astype(F32)
            low = mixed - high
            for at in range(8):
                lanes = slice(at // 4 * 128, at // 4 * 128 + 128)
                rows = slice(d * 256 + at * GW, d * 256 + at * GW + GW)
                mix[0, rows, lanes] = jnp.where(group == at % 4, high[:, lanes], 0.0).astype(BF16)
                mix[1, rows, lanes] = jnp.where(group == at % 4, low[:, lanes], 0.0).astype(BF16)
            begin = REACH + shifts[a, s]
            for p in range(2):
                for h in range(2):
                    lanes = slice(d * 256 + h * 128, d * 256 + h * 128 + 128)
                    taps[p * ROWS : p * ROWS + ROWS, lanes] = f[p, h, a + d, pl.ds(begin, ROWS), :].astype(BF16)

    def gather(a, taps, mix):
        both = jnp.dot(taps[...], mix[0], preferred_element_type=F32)
        total = both[:ROWS] + both[ROWS:]
        total += jnp.dot(taps[0:ROWS, :], mix[1], preferred_element_type=F32)
        conv[a] = conv[a] + total[:SLAB]

    conv[...] = jnp.zeros(conv.shape, F32)
    fill(0, 0, taps_a, mix_a)

    def two_quarters(i, carry):
        second = 2 * i + 1
        fill(second // 4, lax.rem(second, 4), taps_b, mix_b)
        gather(i // 2, taps_a, mix_a)
        third = jnp.minimum(2 * i + 2, 15)
        fill(third // 4, lax.rem(third, 4), taps_a, mix_a)
        gather(second // 4, taps_b, mix_b)
        return carry

    lax.fori_loop(0, 8, two_quarters, 0)

    own.wait()
    everyone = r.at[pl.ds(0, 63)]
    pltpu.make_async_copy(everyone, everyone, s3_recv).wait()
    block = lax.broadcasted_iota(jnp.int32, (32, 128), 1) // 32
    for quad in range(8):
        parts = [r[0:32, quad * 4 + i, :] + r[32:64, quad * 4 + i, :] for i in range(4)]
        turned = jnp.concatenate(parts, axis=0).T
        rows = [turned[a * 32 : a * 32 + 32, :] for a in range(4)]
        made = []
        for i in range(4):
            one = rows[i]
            for a in range(4):
                if a != i:
                    one = jnp.where(block == a, pltpu.roll(rows[a], ((a - i) * 32) % 128, 1), one)
            made.append(one)
        high, low = split(jnp.concatenate(made, axis=0))
        for n in range(2):
            order = ORDER_OF[quad * 2 + n]
            lhs[order, 0:64, :] = high[n * 64 : n * 64 + 64]
            lhs[order, 64:128, :] = low[n * 64 : n * 64 + 64]

    for copy in sends:
        copy.wait_send()
    for copy in edges:
        copy.wait_send()

    @pl.when(lat < 31)
    def _():
        for pair in halo:
            pair[0].wait_send()

    @pl.when(lat > 0)
    def _():
        for pair in halo:
            pair[1].wait_send()

    pltpu.make_async_copy(everyone, everyone, s3_send).wait()


def legendre_kernel(lhs, lp, conv, out, moved, made, out_sem, move_sem):
    moves = [pltpu.make_async_copy(conv.at[a], moved.at[:, a, :], move_sem.at[a]) for a in range(4)]
    for copy in moves:
        copy.start()

    def leaving(m):
        return pltpu.make_async_copy(made.at[m], out.at[m], out_sem.at[m])

    def order(m, carry):
        top, bottom = lhs[m, 0:64, :], lhs[m, 64:128, :]
        left = jnp.concatenate(
            [
                jnp.concatenate([top, top], axis=1),
                jnp.concatenate([bottom, jnp.zeros_like(bottom)], axis=1),
            ],
            axis=0,
        )
        both = jnp.dot(left, lp[m], preferred_element_type=F32)
        made[m] = both[0:64] + both[64:128]
        leaving(m).start()
        return carry

    lax.fori_loop(0, 16, order, 0, unroll=4)
    for copy in moves:
        copy.wait()
    lax.fori_loop(0, 16, lambda m, carry: leaving(m).wait(), None)


def shards(field, legendre, shifts, psi, kernel_weight):
    even, odd = fourier_tables()
    vmem = pl.BlockSpec(memory_space=pltpu.VMEM)
    hbm = pl.BlockSpec(memory_space=pltpu.HBM)
    dma = pltpu.SemaphoreType.DMA
    conv, lhs, prepared = pl.pallas_call(
        main_kernel,
        out_shape=(
            pltpu.VMEM((4, SLAB, 256), F32),
            pltpu.VMEM((16, 128, 128), BF16),
            pltpu.VMEM((16, 256, 720), BF16),
        ),
        in_specs=[hbm] * 7,
        out_specs=(vmem, vmem, vmem),
        scratch_shapes=[
            pltpu.VMEM((4, SLAB, 256), F32),
            pltpu.VMEM((2, 2, SLAB, 256), F32),
            pltpu.VMEM((2, 8, REACH, 256), F32),
            pltpu.VMEM((2, 2, 8, SPAN, 128), F32),
            pltpu.VMEM((8, PAD, 128), F32),
            pltpu.VMEM((2, 4, PAD, 128), F32),
            pltpu.VMEM((2, 32, 32, 128), F32),
            pltpu.VMEM((64, 32, 128), F32),
            pltpu.VMEM((2 * ROWS, STRIDE * 256), BF16),
            pltpu.VMEM((2 * ROWS, STRIDE * 256), BF16),
            pltpu.VMEM((2, STRIDE * 256, 256), BF16),
            pltpu.VMEM((2, STRIDE * 256, 256), BF16),
            pltpu.VMEM((2, 512, PAD), BF16),
            pltpu.VMEM((2, 512, 2 * PAD), BF16),
            pltpu.VMEM((2, 4, REACH, 256), F32),
            pltpu.VMEM((KERNELS, GW, 256), F32),
            pltpu.VMEM((16, 720, 128), F32),
            pltpu.VMEM((6, 128, 128), F32),
            pltpu.SMEM((4, SLOTS), jnp.int32),
            pltpu.SMEM((KERNELS, 4, SLOTS), F32),
            dma((4,)),
            dma((6,)),
            dma((2, 3)),
            dma((2, 3)),
            dma((2,)),
            dma((2,)),
            dma((3, 2)),
            dma((3, 2)),
            dma,
            dma,
            dma,
        ],
        compiler_params=pltpu.CompilerParams(
            collective_id=0, has_side_effects=True, vmem_limit_bytes=44 * 1024 * 1024
        ),
        cost_estimate=pl.CostEstimate(flops=4_000_000_000, bytes_accessed=8_000_000, transcendentals=0),
        name="spectrum_and_convolution",
    )(
        *(
            pltpu.with_memory_space_constraint(value, pltpu.HBM)
            for value in (
                shifts,
                psi.transpose(2, 0, 1),
                field.transpose(1, 0, 2),
                kernel_weight,
                jnp.asarray(even),
                jnp.asarray(odd),
                legendre,
            )
        )
    )
    coefficients, moved = pl.pallas_call(
        legendre_kernel,
        out_shape=(
            jax.ShapeDtypeStruct((16, 64, 720), F32),
            jax.ShapeDtypeStruct((SLAB, 4, 256), F32),
        ),
        in_specs=[vmem, vmem, vmem],
        out_specs=(hbm, hbm),
        scratch_shapes=[pltpu.VMEM((16, 64, 720), F32), dma((16,)), dma((4,))],
        compiler_params=pltpu.CompilerParams(vmem_limit_bytes=24 * 1024 * 1024),
        cost_estimate=pl.CostEstimate(flops=800_000_000, bytes_accessed=10_000_000, transcendentals=0),
        name="legendre",
    )(lhs, prepared, conv)
    coefficients = coefficients.reshape(16, 2, GW, 720).transpose(0, 3, 1, 2)
    return coefficients, moved.transpose(1, 0, 2)


def solution(mesh):
    placed = (
        P("lat", "lon", None),
        P("lat", None, None),
        P("lat", None),
        P("lat", None, None),
        P(),
    )
    return jax.shard_map(
        shards,
        mesh=mesh,
        in_specs=placed,
        out_specs=(P("lat", None, None, "lon"), P("lat", "lon", None)),
        check_vma=False,
    )
```

```python
import jax
import jax.numpy as jnp
import ml_dtypes
import numpy as np
from jax import lax
from jax.experimental import pallas as pl
from jax.experimental.pallas import tpu as pltpu
from jax.sharding import PartitionSpec as P

LON = 1440
ORDERS = 512
SLAB = 180
PAD = 184
GW = 32
KERNELS = 9
SLOTS = 20
RADIUS = 2
REACH = 16
STRIDE = 2 * RADIUS + 1
ROWS = 192
SPAN = 232
MESH = pl.DeviceIdType.MESH
F32 = jnp.float32
BF16 = jnp.bfloat16
ORDER_OF = [0, 4, 8, 12, 2, 6, 10, 14, 1, 3, 5, 7, 9, 11, 13, 15]


def two_parts(table):
    table = np.asarray(table, np.float32)
    high = table.astype(ml_dtypes.bfloat16)
    low = (table - high.astype(np.float32)).astype(ml_dtypes.bfloat16)
    return np.stack([high, low])


def fourier_tables():
    even, odd = [], []
    for half in range(2):
        j = SLAB * half + np.arange(PAD)
        live = (np.arange(PAD) < SLAB).astype(np.float64)

        def rows(orders, lead):
            turn = (np.asarray(orders)[:, None] * (j[None, :] + lead)) % LON
            angle = turn * (2.0 * np.pi / LON)
            both = np.stack([np.cos(angle), -np.sin(angle)], axis=1) * live
            return both.reshape(-1, PAD)

        owner = np.arange(32)[:, None] * 16
        zero = (owner + np.arange(0, 16, 4)).reshape(-1)
        two = (owner + np.arange(2, 16, 4)).reshape(-1)
        ones = (owner + np.arange(1, 16, 2)).reshape(-1)
        even.append(two_parts(np.concatenate([rows(zero, 0), rows(two, 0)])))
        odd.append(two_parts(np.concatenate([rows(ones, 0), rows(ones, 360)], axis=1)))
    return np.stack(even), np.stack(odd)


def split(value):
    high = value.astype(BF16)
    return high, (value - high.astype(F32)).astype(BF16)


def main_kernel(
    shifts_in, psi_in, field, weight_in, even, odd, legendre,
    conv, lhs, lp,
    g, gh_rows, e, f, pk, xr, sp, r, taps_a, taps_b, mix_a, mix_b, te, to, es, weight, lf, turned_l, shifts, psi,
    load_sem, table_sem, s1_send, s1_recv, h_send, h_recv, c_send, c_recv, s3_send, s3_recv, own_sem,
):
    lat = lax.axis_index("lat")
    lon = lax.axis_index("lon")
    x, half = lon // 2, lon % 2
    z_lo, y, core = lat // 8, (lat // 2) % 4, lat % 2
    right = lax.rem(lon + 1, 8)
    left = lax.rem(lon + 7, 8)

    loads = [
        pltpu.make_async_copy(field.at[:, a, :], g.at[a], load_sem.at[a])
        for a in range(4)
    ]
    tables = [
        pltpu.make_async_copy(weight_in, weight, table_sem.at[0]),
        pltpu.make_async_copy(even.at[half], te, table_sem.at[1]),
        pltpu.make_async_copy(odd.at[half], to, table_sem.at[2]),
        pltpu.make_async_copy(psi_in, psi, table_sem.at[3]),
        pltpu.make_async_copy(shifts_in, shifts, table_sem.at[4]),
        pltpu.make_async_copy(legendre, lf, table_sem.at[5]),
    ]
    for copy in loads + tables:
        copy.start()
    pk[:, SLAB:PAD, :] = jnp.zeros((8, PAD - SLAB, 128), F32)

    barrier = pltpu.get_barrier_semaphore()

    def greet(step, carry):
        peer = lax.rem(lat + lax.rem(step, 32), 32)
        column = 2 * x + lax.rem(half + step // 32, 2)
        pl.semaphore_signal(barrier, inc=1, device_id=(peer, column), device_id_type=MESH)
        return carry

    lax.fori_loop(1, 64, greet, 0)
    for step in range(1, 4):
        pl.semaphore_signal(
            barrier, inc=1, device_id=(lat, 2 * lax.rem(x + step, 4) + half), device_id_type=MESH
        )
    outer = jnp.where(half == 1, right, left)
    pl.semaphore_signal(barrier, inc=1, device_id=(lat, outer), device_id_type=MESH)

    for copy in loads:
        copy.wait()
    es[0] = g[:, 0:REACH, :]
    es[1] = g[:, SLAB - REACH : SLAB, :]
    def pack(at, count, parity):
        lane_block = lax.broadcasted_iota(jnp.int32, (count, 128), 1) // 32
        for tile in range(2):
            rows = [g[a, at, tile * 128 : tile * 128 + 128] for a in range(4)]
            for q in (parity, parity + 2):
                made = rows[q]
                for a in range(4):
                    if a != q:
                        moved = pltpu.roll(rows[a], ((a - q) * 32) % 128, 1)
                        made = jnp.where(lane_block == a, moved, made)
                pk[tile * 4 + q, at, :] = made

    def pack_half(parity):
        def strip(at, carry):
            pack(pl.ds(pl.multiple_of(at * 8, 8), 8), 8, parity)
            return carry

        lax.fori_loop(0, SLAB // 8, strip, 0, unroll=2)
        pack(pl.ds(SLAB - 4, 4), 4, parity)

    @pl.when(half == 0)
    def _():
        pack_half(1)

    @pl.when(half == 1)
    def _():
        pack_half(0)

    pl.semaphore_wait(barrier, 63 + 3 + 1)

    def exchange(turn):
        chunk = lax.rem(half + 1 + turn, 2)
        copies = []
        for step in (2, 1, 3):
            there = lax.rem(x + step, 4)
            copy = pltpu.make_async_remote_copy(
                src_ref=pk.at[2 * there + chunk],
                dst_ref=xr.at[turn, x],
                send_sem=s1_send.at[turn, step - 1],
                recv_sem=s1_recv.at[turn, step - 1],
                device_id=(lat, 2 * there + half),
                device_id_type=MESH,
            )
            copy.start()
            copies.append(copy)
        return copies

    sends = exchange(0)
    edges = []
    for side, there in ((1, left), (0, right)):
        copy = pltpu.make_async_remote_copy(
            src_ref=es.at[1 - side],
            dst_ref=e.at[side, pl.ds(2, 4)],
            send_sem=h_send.at[side],
            recv_sem=h_recv.at[side],
            device_id=(lat, there),
            device_id_type=MESH,
        )
        copy.start()
        edges.append(copy)
    up, down = lax.rem(lat + 1, 32), lax.rem(lat + 31, 32)

    def row_copies(rows, above, below, send, recv):
        return (
            pltpu.make_async_remote_copy(
                src_ref=rows.at[pl.ds(2, 2)], dst_ref=above,
                send_sem=send.at[0], recv_sem=recv.at[0],
                device_id=(up, lon), device_id_type=MESH,
            ),
            pltpu.make_async_remote_copy(
                src_ref=rows.at[pl.ds(0, 2)], dst_ref=below,
                send_sem=send.at[1], recv_sem=recv.at[1],
                device_id=(down, lon), device_id_type=MESH,
            ),
        )

    halo = [row_copies(g, gh_rows.at[0], gh_rows.at[1], c_send.at[0], c_recv.at[0])] + [
        row_copies(
            e.at[side, pl.ds(2, 4)], e.at[side, pl.ds(0, 2)], e.at[side, pl.ds(6, 2)],
            c_send.at[1 + side], c_recv.at[1 + side],
        )
        for side in range(2)
    ]

    def start_rows(pair):
        @pl.when(lat < 31)
        def _():
            pair[0].start()

        @pl.when(lat > 0)
        def _():
            pair[1].start()

    start_rows(halo[0])

    @pl.when(half == 0)
    def _():
        pack_half(0)

    @pl.when(half == 1)
    def _():
        pack_half(1)

    sends += exchange(1)
    for turn in range(2):
        chunk = lax.rem(half + 1 + turn, 2)
        xr[turn, x] = pk[2 * x + chunk]

    @pl.when(lat == 0)
    def _():
        gh_rows[0] = jnp.zeros((2, SLAB, 256), F32)
        e[:, 0:2] = jnp.zeros((2, 2, REACH, 256), F32)

    @pl.when(lat == 31)
    def _():
        gh_rows[1] = jnp.zeros((2, SLAB, 256), F32)
        e[:, 6:8] = jnp.zeros((2, 2, REACH, 256), F32)

    mix_a[...] = jnp.zeros(mix_a.shape, BF16)
    mix_b[...] = jnp.zeros(mix_b.shape, BF16)
    tables[5].wait()

    def prepare(m, carry):
        for block in range(6):
            count = min(128, 720 - block * 128)
            columns = slice(block * 128, block * 128 + count)
            turned_l[block, :, 0:count] = lf[m, columns, :].T
            for a in range(4):
                high, low = split(turned_l[block, pl.ds(a, 32, stride=4), :])
                lp[m, a * 32 : a * 32 + 32, columns] = high[:, :count]
                lp[m, 128 + a * 32 : 160 + a * 32, columns] = low[:, :count]
        return carry

    lax.fori_loop(0, 16, prepare, 0, unroll=2)

    tables[1].wait()
    tables[2].wait()

    def transform(turn):
        s0, s1, s2, s3 = (xr[turn, i] for i in range(4))
        p02, p13 = s0 + s2, s1 + s3
        for at, value in ((0, p02 + p13), (1, p02 - p13)):
            high, low = split(value)
            both = jnp.concatenate([high, low], axis=1)
            rows = pl.ds(at * 256, 256)
            first = jnp.dot(te[0, rows, :], both, preferred_element_type=F32)
            second = jnp.dot(te[1, rows, :], high, preferred_element_type=F32)
            total = first[:, :128] + first[:, 128:] + second
            sp[turn, :, at * 8 : at * 8 + 8, :] = total.reshape(32, 8, 128)
        high, low = split(jnp.concatenate([s0 - s2, s1 - s3], axis=0))
        both = jnp.concatenate([high, low], axis=1)
        first = jnp.dot(to[0], both, preferred_element_type=F32)
        second = jnp.dot(to[1], high, preferred_element_type=F32)
        total = first[:, :128] + first[:, 128:] + second
        sp[turn, :, 16:32, :] = total.reshape(32, 16, 128)

    mine = half * 32 + lat

    def scatter(turn):
        column = 2 * x + lax.rem(half + 1 + turn, 2)

        def send(step, carry):
            there = (
                lax.rem(z_lo + lax.rem(step, 4), 4) * 8
                + lax.rem(y + lax.rem(step, 32) // 8, 4) * 2
                + lax.rem(core + step // 4, 2)
            )
            pltpu.make_async_remote_copy(
                src_ref=sp.at[turn, there],
                dst_ref=r.at[mine],
                send_sem=s3_send,
                recv_sem=s3_recv,
                device_id=(there, column),
                device_id_type=MESH,
            ).start()
            return carry

        lax.fori_loop(turn, 32, send, 0)

    for turn in range(2):
        for copy in sends[turn * 3 : turn * 3 + 3]:
            copy.wait_recv()
        transform(turn)
        if turn == 0:
            for copy in edges:
                copy.wait_recv()
            start_rows(halo[1])
            start_rows(halo[2])
        scatter(turn)
    own = pltpu.make_async_copy(sp.at[1, lat], r.at[mine], own_sem)
    own.start()

    @pl.when(lat > 0)
    def _():
        for pair in halo:
            pair[0].wait_recv()

    @pl.when(lat < 31)
    def _():
        for pair in halo:
            pair[1].wait_recv()

    def place(row, h, at, value):
        high = value.astype(BF16).astype(F32)
        f[0, h, row, at : at + value.shape[0], :] = high
        f[1, h, row, at : at + value.shape[0], :] = value - high

    for row in range(8):
        source = g.at[row - 2] if 2 <= row < 6 else gh_rows.at[row // 6, row % 2]
        for h in range(2):
            lanes = slice(h * 128, h * 128 + 128)
            place(row, h, 0, e[0, row, :, lanes])
            place(row, h, REACH, source[:, lanes])
            place(row, h, REACH + SLAB, e[1, row, :, lanes])
            f[:, h, row, 2 * REACH + SLAB : SPAN, :] = jnp.zeros((2, SPAN - 2 * REACH - SLAB, 128), F32)

    for table in (tables[0], tables[3], tables[4]):
        table.wait()
    group = lax.broadcasted_iota(jnp.int32, (GW, 128), 1) // GW

    def fill(a, quarter, taps, mix):
        for d in range(STRIDE):
            s = quarter * STRIDE + d
            mixed = psi[0, a, s] * weight[0]
            for k in range(1, KERNELS):
                mixed = mixed + psi[k, a, s] * weight[k]
            high = mixed.astype(BF16).astype(F32)
            low = mixed - high
            for at in range(8):
                lanes = slice(at // 4 * 128, at // 4 * 128 + 128)
                rows = slice(d * 256 + at * GW, d * 256 + at * GW + GW)
                mix[0, rows, lanes] = jnp.where(group == at % 4, high[:, lanes], 0.0).astype(BF16)
                mix[1, rows, lanes] = jnp.where(group == at % 4, low[:, lanes], 0.0).astype(BF16)
            begin = REACH + shifts[a, s]
            for p in range(2):
                for h in range(2):
                    lanes = slice(d * 256 + h * 128, d * 256 + h * 128 + 128)
                    taps[p * ROWS : p * ROWS + ROWS, lanes] = f[p, h, a + d, pl.ds(begin, ROWS), :].astype(BF16)

    def gather(a, taps, mix):
        both = jnp.dot(taps[...], mix[0], preferred_element_type=F32)
        total = both[:ROWS] + both[ROWS:]
        total += jnp.dot(taps[0:ROWS, :], mix[1], preferred_element_type=F32)
        conv[a] = conv[a] + total[:SLAB]

    conv[...] = jnp.zeros(conv.shape, F32)
    fill(0, 0, taps_a, mix_a)

    def two_quarters(i, carry):
        second = 2 * i + 1
        fill(second // 4, lax.rem(second, 4), taps_b, mix_b)
        gather(i // 2, taps_a, mix_a)
        third = jnp.minimum(2 * i + 2, 15)
        fill(third // 4, lax.rem(third, 4), taps_a, mix_a)
        gather(second // 4, taps_b, mix_b)
        return carry

    lax.fori_loop(0, 8, two_quarters, 0)

    own.wait()
    everyone = r.at[pl.ds(0, 63)]
    pltpu.make_async_copy(everyone, everyone, s3_recv).wait()
    block = lax.broadcasted_iota(jnp.int32, (32, 128), 1) // 32
    for quad in range(8):
        parts = [r[0:32, quad * 4 + i, :] + r[32:64, quad * 4 + i, :] for i in range(4)]
        turned = jnp.concatenate(parts, axis=0).T
        rows = [turned[a * 32 : a * 32 + 32, :] for a in range(4)]
        made = []
        for i in range(4):
            one = rows[i]
            for a in range(4):
                if a != i:
                    one = jnp.where(block == a, pltpu.roll(rows[a], ((a - i) * 32) % 128, 1), one)
            made.append(one)
        high, low = split(jnp.concatenate(made, axis=0))
        for n in range(2):
            order = ORDER_OF[quad * 2 + n]
            lhs[order, 0:64, :] = high[n * 64 : n * 64 + 64]
            lhs[order, 64:128, :] = low[n * 64 : n * 64 + 64]

    for copy in sends:
        copy.wait_send()
    for copy in edges:
        copy.wait_send()

    @pl.when(lat < 31)
    def _():
        for pair in halo:
            pair[0].wait_send()

    @pl.when(lat > 0)
    def _():
        for pair in halo:
            pair[1].wait_send()

    pltpu.make_async_copy(everyone, everyone, s3_send).wait()


def legendre_kernel(lhs, lp, conv, out, moved, made, out_sem, move_sem):
    moves = [pltpu.make_async_copy(conv.at[a], moved.at[:, a, :], move_sem.at[a]) for a in range(4)]
    for copy in moves:
        copy.start()

    def leaving(m):
        return pltpu.make_async_copy(made.at[m], out.at[m], out_sem.at[m])

    def order(m, carry):
        top, bottom = lhs[m, 0:64, :], lhs[m, 64:128, :]
        left = jnp.concatenate(
            [
                jnp.concatenate([top, top], axis=1),
                jnp.concatenate([bottom, jnp.zeros_like(bottom)], axis=1),
            ],
            axis=0,
        )
        both = jnp.dot(left, lp[m], preferred_element_type=F32)
        made[m] = both[0:64] + both[64:128]
        leaving(m).start()
        return carry

    lax.fori_loop(0, 16, order, 0, unroll=16)
    for copy in moves:
        copy.wait()
    lax.fori_loop(0, 16, lambda m, carry: leaving(m).wait(), None)


def shards(field, legendre, shifts, psi, kernel_weight):
    even, odd = fourier_tables()
    vmem = pl.BlockSpec(memory_space=pltpu.VMEM)
    hbm = pl.BlockSpec(memory_space=pltpu.HBM)
    dma = pltpu.SemaphoreType.DMA
    conv, lhs, prepared = pl.pallas_call(
        main_kernel,
        out_shape=(
            pltpu.VMEM((4, SLAB, 256), F32),
            pltpu.VMEM((16, 128, 128), BF16),
            pltpu.VMEM((16, 256, 720), BF16),
        ),
        in_specs=[hbm] * 7,
        out_specs=(vmem, vmem, vmem),
        scratch_shapes=[
            pltpu.VMEM((4, SLAB, 256), F32),
            pltpu.VMEM((2, 2, SLAB, 256), F32),
            pltpu.VMEM((2, 8, REACH, 256), F32),
            pltpu.VMEM((2, 2, 8, SPAN, 128), F32),
            pltpu.VMEM((8, PAD, 128), F32),
            pltpu.VMEM((2, 4, PAD, 128), F32),
            pltpu.VMEM((2, 32, 32, 128), F32),
            pltpu.VMEM((64, 32, 128), F32),
            pltpu.VMEM((2 * ROWS, STRIDE * 256), BF16),
            pltpu.VMEM((2 * ROWS, STRIDE * 256), BF16),
            pltpu.VMEM((2, STRIDE * 256, 256), BF16),
            pltpu.VMEM((2, STRIDE * 256, 256), BF16),
            pltpu.VMEM((2, 512, PAD), BF16),
            pltpu.VMEM((2, 512, 2 * PAD), BF16),
            pltpu.VMEM((2, 4, REACH, 256), F32),
            pltpu.VMEM((KERNELS, GW, 256), F32),
            pltpu.VMEM((16, 720, 128), F32),
            pltpu.VMEM((6, 128, 128), F32),
            pltpu.SMEM((4, SLOTS), jnp.int32),
            pltpu.SMEM((KERNELS, 4, SLOTS), F32),
            dma((4,)),
            dma((6,)),
            dma((2, 3)),
            dma((2, 3)),
            dma((2,)),
            dma((2,)),
            dma((3, 2)),
            dma((3, 2)),
            dma,
            dma,
            dma,
        ],
        compiler_params=pltpu.CompilerParams(
            collective_id=0, has_side_effects=True, vmem_limit_bytes=44 * 1024 * 1024
        ),
        cost_estimate=pl.CostEstimate(flops=4_000_000_000, bytes_accessed=8_000_000, transcendentals=0),
        name="spectrum_and_convolution",
    )(
        *(
            pltpu.with_memory_space_constraint(value, pltpu.HBM)
            for value in (
                shifts,
                psi.transpose(2, 0, 1),
                field.transpose(1, 0, 2),
                kernel_weight,
                jnp.asarray(even),
                jnp.asarray(odd),
                legendre,
            )
        )
    )
    coefficients, moved = pl.pallas_call(
        legendre_kernel,
        out_shape=(
            jax.ShapeDtypeStruct((16, 64, 720), F32),
            jax.ShapeDtypeStruct((SLAB, 4, 256), F32),
        ),
        in_specs=[vmem, vmem, vmem],
        out_specs=(hbm, hbm),
        scratch_shapes=[pltpu.VMEM((16, 64, 720), F32), dma((16,)), dma((4,))],
        compiler_params=pltpu.CompilerParams(vmem_limit_bytes=24 * 1024 * 1024),
        cost_estimate=pl.CostEstimate(flops=800_000_000, bytes_accessed=10_000_000, transcendentals=0),
        name="legendre",
    )(lhs, prepared, conv)
    coefficients = coefficients.reshape(16, 2, GW, 720).transpose(0, 3, 1, 2)
    return coefficients, moved.transpose(1, 0, 2)


def solution(mesh):
    placed = (
        P("lat", "lon", None),
        P("lat", None, None),
        P("lat", None),
        P("lat", None, None),
        P(),
    )
    return jax.shard_map(
        shards,
        mesh=mesh,
        in_specs=placed,
        out_specs=(P("lat", None, None, "lon"), P("lat", "lon", None)),
        check_vma=False,
    )
```

```python
import jax
import jax.numpy as jnp
import ml_dtypes
import numpy as np
from jax import lax
from jax.experimental import pallas as pl
from jax.experimental.pallas import tpu as pltpu
from jax.sharding import PartitionSpec as P

LON = 1440
ORDERS = 512
SLAB = 180
PAD = 184
GW = 32
KERNELS = 9
SLOTS = 20
RADIUS = 2
REACH = 16
STRIDE = 2 * RADIUS + 1
ROWS = 192
SPAN = 232
MESH = pl.DeviceIdType.MESH
F32 = jnp.float32
BF16 = jnp.bfloat16
ORDER_OF = [0, 4, 8, 12, 2, 6, 10, 14, 1, 3, 5, 7, 9, 11, 13, 15]


def two_parts(table):
    table = np.asarray(table, np.float32)
    high = table.astype(ml_dtypes.bfloat16)
    low = (table - high.astype(np.float32)).astype(ml_dtypes.bfloat16)
    return np.stack([high, low])


def fourier_tables():
    even, odd = [], []
    for half in range(2):
        j = SLAB * half + np.arange(PAD)
        live = (np.arange(PAD) < SLAB).astype(np.float64)

        def rows(orders, lead):
            turn = (np.asarray(orders)[:, None] * (j[None, :] + lead)) % LON
            angle = turn * (2.0 * np.pi / LON)
            both = np.stack([np.cos(angle), -np.sin(angle)], axis=1) * live
            return both.reshape(-1, PAD)

        owner = np.arange(32)[:, None] * 16
        zero = (owner + np.arange(0, 16, 4)).reshape(-1)
        two = (owner + np.arange(2, 16, 4)).reshape(-1)
        ones = (owner + np.arange(1, 16, 2)).reshape(-1)
        even.append(two_parts(np.concatenate([rows(zero, 0), rows(two, 0)])))
        odd.append(two_parts(np.concatenate([rows(ones, 0), rows(ones, 360)], axis=1)))
    return np.stack(even), np.stack(odd)


def split(value):
    high = value.astype(BF16)
    return high, (value - high.astype(F32)).astype(BF16)


def main_kernel(
    shifts_in, psi_in, field, weight_in, even, odd, legendre,
    conv, lhs, lp,
    g, gh_rows, e, f, pk, xr, sp, r, taps_a, taps_b, mix_a, mix_b, te, to, es, weight, lf, turned_l, shifts, psi,
    load_sem, table_sem, s1_send, s1_recv, h_send, h_recv, c_send, c_recv, s3_send, s3_recv, own_sem,
):
    lat = lax.axis_index("lat")
    lon = lax.axis_index("lon")
    x, half = lon // 2, lon % 2
    z_lo, y, core = lat // 8, (lat // 2) % 4, lat % 2
    right = lax.rem(lon + 1, 8)
    left = lax.rem(lon + 7, 8)

    loads = [
        pltpu.make_async_copy(field.at[:, a, :], g.at[a], load_sem.at[a])
        for a in range(4)
    ]
    tables = [
        pltpu.make_async_copy(weight_in, weight, table_sem.at[0]),
        pltpu.make_async_copy(even.at[half], te, table_sem.at[1]),
        pltpu.make_async_copy(odd.at[half], to, table_sem.at[2]),
        pltpu.make_async_copy(psi_in, psi, table_sem.at[3]),
        pltpu.make_async_copy(shifts_in, shifts, table_sem.at[4]),
        pltpu.make_async_copy(legendre, lf, table_sem.at[5]),
    ]
    for copy in loads:
        copy.start()
    pk[:, SLAB:PAD, :] = jnp.zeros((8, PAD - SLAB, 128), F32)

    barrier = pltpu.get_barrier_semaphore()

    def greet(step, carry):
        peer = lax.rem(lat + lax.rem(step, 32), 32)
        column = 2 * x + lax.rem(half + step // 32, 2)
        pl.semaphore_signal(barrier, inc=1, device_id=(peer, column), device_id_type=MESH)
        return carry

    lax.fori_loop(1, 64, greet, 0)
    for step in range(1, 4):
        pl.semaphore_signal(
            barrier, inc=1, device_id=(lat, 2 * lax.rem(x + step, 4) + half), device_id_type=MESH
        )
    outer = jnp.where(half == 1, right, left)
    pl.semaphore_signal(barrier, inc=1, device_id=(lat, outer), device_id_type=MESH)

    for copy in loads:
        copy.wait()
    for copy in tables:
        copy.start()
    es[0] = g[:, 0:REACH, :]
    es[1] = g[:, SLAB - REACH : SLAB, :]
    def pack(at, count, parity):
        lane_block = lax.broadcasted_iota(jnp.int32, (count, 128), 1) // 32
        for tile in range(2):
            rows = [g[a, at, tile * 128 : tile * 128 + 128] for a in range(4)]
            for q in (parity, parity + 2):
                made = rows[q]
                for a in range(4):
                    if a != q:
                        moved = pltpu.roll(rows[a], ((a - q) * 32) % 128, 1)
                        made = jnp.where(lane_block == a, moved, made)
                pk[tile * 4 + q, at, :] = made

    def pack_half(parity):
        def strip(at, carry):
            pack(pl.ds(pl.multiple_of(at * 8, 8), 8), 8, parity)
            return carry

        lax.fori_loop(0, SLAB // 8, strip, 0, unroll=2)
        pack(pl.ds(SLAB - 4, 4), 4, parity)

    @pl.when(half == 0)
    def _():
        pack_half(1)

    @pl.when(half == 1)
    def _():
        pack_half(0)

    pl.semaphore_wait(barrier, 63 + 3 + 1)

    def exchange(turn):
        chunk = lax.rem(half + 1 + turn, 2)
        copies = []
        for step in (2, 1, 3):
            there = lax.rem(x + step, 4)
            copy = pltpu.make_async_remote_copy(
                src_ref=pk.at[2 * there + chunk],
                dst_ref=xr.at[turn, x],
                send_sem=s1_send.at[turn, step - 1],
                recv_sem=s1_recv.at[turn, step - 1],
                device_id=(lat, 2 * there + half),
                device_id_type=MESH,
            )
            copy.start()
            copies.append(copy)
        return copies

    sends = exchange(0)
    edges = []
    for side, there in ((1, left), (0, right)):
        copy = pltpu.make_async_remote_copy(
            src_ref=es.at[1 - side],
            dst_ref=e.at[side, pl.ds(2, 4)],
            send_sem=h_send.at[side],
            recv_sem=h_recv.at[side],
            device_id=(lat, there),
            device_id_type=MESH,
        )
        copy.start()
        edges.append(copy)
    up, down = lax.rem(lat + 1, 32), lax.rem(lat + 31, 32)

    def row_copies(rows, above, below, send, recv):
        return (
            pltpu.make_async_remote_copy(
                src_ref=rows.at[pl.ds(2, 2)], dst_ref=above,
                send_sem=send.at[0], recv_sem=recv.at[0],
                device_id=(up, lon), device_id_type=MESH,
            ),
            pltpu.make_async_remote_copy(
                src_ref=rows.at[pl.ds(0, 2)], dst_ref=below,
                send_sem=send.at[1], recv_sem=recv.at[1],
                device_id=(down, lon), device_id_type=MESH,
            ),
        )

    halo = [row_copies(g, gh_rows.at[0], gh_rows.at[1], c_send.at[0], c_recv.at[0])] + [
        row_copies(
            e.at[side, pl.ds(2, 4)], e.at[side, pl.ds(0, 2)], e.at[side, pl.ds(6, 2)],
            c_send.at[1 + side], c_recv.at[1 + side],
        )
        for side in range(2)
    ]

    def start_rows(pair):
        @pl.when(lat < 31)
        def _():
            pair[0].start()

        @pl.when(lat > 0)
        def _():
            pair[1].start()

    start_rows(halo[0])

    @pl.when(half == 0)
    def _():
        pack_half(0)

    @pl.when(half == 1)
    def _():
        pack_half(1)

    sends += exchange(1)
    for turn in range(2):
        chunk = lax.rem(half + 1 + turn, 2)
        xr[turn, x] = pk[2 * x + chunk]

    @pl.when(lat == 0)
    def _():
        gh_rows[0] = jnp.zeros((2, SLAB, 256), F32)
        e[:, 0:2] = jnp.zeros((2, 2, REACH, 256), F32)

    @pl.when(lat == 31)
    def _():
        gh_rows[1] = jnp.zeros((2, SLAB, 256), F32)
        e[:, 6:8] = jnp.zeros((2, 2, REACH, 256), F32)

    mix_a[...] = jnp.zeros(mix_a.shape, BF16)
    mix_b[...] = jnp.zeros(mix_b.shape, BF16)
    tables[5].wait()

    def prepare(m, carry):
        for block in range(6):
            count = min(128, 720 - block * 128)
            columns = slice(block * 128, block * 128 + count)
            turned_l[block, :, 0:count] = lf[m, columns, :].T
            for a in range(4):
                high, low = split(turned_l[block, pl.ds(a, 32, stride=4), :])
                lp[m, a * 32 : a * 32 + 32, columns] = high[:, :count]
                lp[m, 128 + a * 32 : 160 + a * 32, columns] = low[:, :count]
        return carry

    lax.fori_loop(0, 16, prepare, 0, unroll=2)

    tables[1].wait()
    tables[2].wait()

    def transform(turn):
        s0, s1, s2, s3 = (xr[turn, i] for i in range(4))
        p02, p13 = s0 + s2, s1 + s3
        for at, value in ((0, p02 + p13), (1, p02 - p13)):
            high, low = split(value)
            both = jnp.concatenate([high, low], axis=1)
            rows = pl.ds(at * 256, 256)
            first = jnp.dot(te[0, rows, :], both, preferred_element_type=F32)
            second = jnp.dot(te[1, rows, :], high, preferred_element_type=F32)
            total = first[:, :128] + first[:, 128:] + second
            sp[turn, :, at * 8 : at * 8 + 8, :] = total.reshape(32, 8, 128)
        high, low = split(jnp.concatenate([s0 - s2, s1 - s3], axis=0))
        both = jnp.concatenate([high, low], axis=1)
        first = jnp.dot(to[0], both, preferred_element_type=F32)
        second = jnp.dot(to[1], high, preferred_element_type=F32)
        total = first[:, :128] + first[:, 128:] + second
        sp[turn, :, 16:32, :] = total.reshape(32, 16, 128)

    mine = half * 32 + lat

    def scatter(turn):
        column = 2 * x + lax.rem(half + 1 + turn, 2)

        def send(step, carry):
            there = (
                lax.rem(z_lo + lax.rem(step, 4), 4) * 8
                + lax.rem(y + lax.rem(step, 32) // 8, 4) * 2
                + lax.rem(core + step // 4, 2)
            )
            pltpu.make_async_remote_copy(
                src_ref=sp.at[turn, there],
                dst_ref=r.at[mine],
                send_sem=s3_send,
                recv_sem=s3_recv,
                device_id=(there, column),
                device_id_type=MESH,
            ).start()
            return carry

        lax.fori_loop(turn, 32, send, 0)

    for turn in range(2):
        for copy in sends[turn * 3 : turn * 3 + 3]:
            copy.wait_recv()
        transform(turn)
        if turn == 0:
            for copy in edges:
                copy.wait_recv()
            start_rows(halo[1])
            start_rows(halo[2])
        scatter(turn)
    own = pltpu.make_async_copy(sp.at[1, lat], r.at[mine], own_sem)
    own.start()

    @pl.when(lat > 0)
    def _():
        for pair in halo:
            pair[0].wait_recv()

    @pl.when(lat < 31)
    def _():
        for pair in halo:
            pair[1].wait_recv()

    def place(row, h, at, value):
        high = value.astype(BF16).astype(F32)
        f[0, h, row, at : at + value.shape[0], :] = high
        f[1, h, row, at : at + value.shape[0], :] = value - high

    for row in range(8):
        source = g.at[row - 2] if 2 <= row < 6 else gh_rows.at[row // 6, row % 2]
        for h in range(2):
            lanes = slice(h * 128, h * 128 + 128)
            place(row, h, 0, e[0, row, :, lanes])
            place(row, h, REACH, source[:, lanes])
            place(row, h, REACH + SLAB, e[1, row, :, lanes])
            f[:, h, row, 2 * REACH + SLAB : SPAN, :] = jnp.zeros((2, SPAN - 2 * REACH - SLAB, 128), F32)

    for table in (tables[0], tables[3], tables[4]):
        table.wait()
    group = lax.broadcasted_iota(jnp.int32, (GW, 128), 1) // GW

    def fill(a, quarter, taps, mix):
        for d in range(STRIDE):
            s = quarter * STRIDE + d
            mixed = psi[0, a, s] * weight[0]
            for k in range(1, KERNELS):
                mixed = mixed + psi[k, a, s] * weight[k]
            high = mixed.astype(BF16).astype(F32)
            low = mixed - high
            for at in range(8):
                lanes = slice(at // 4 * 128, at // 4 * 128 + 128)
                rows = slice(d * 256 + at * GW, d * 256 + at * GW + GW)
                mix[0, rows, lanes] = jnp.where(group == at % 4, high[:, lanes], 0.0).astype(BF16)
                mix[1, rows, lanes] = jnp.where(group == at % 4, low[:, lanes], 0.0).astype(BF16)
            begin = REACH + shifts[a, s]
            for p in range(2):
                for h in range(2):
                    lanes = slice(d * 256 + h * 128, d * 256 + h * 128 + 128)
                    taps[p * ROWS : p * ROWS + ROWS, lanes] = f[p, h, a + d, pl.ds(begin, ROWS), :].astype(BF16)

    def gather(a, taps, mix):
        both = jnp.dot(taps[...], mix[0], preferred_element_type=F32)
        total = both[:ROWS] + both[ROWS:]
        total += jnp.dot(taps[0:ROWS, :], mix[1], preferred_element_type=F32)
        conv[a] = conv[a] + total[:SLAB]

    conv[...] = jnp.zeros(conv.shape, F32)
    fill(0, 0, taps_a, mix_a)

    def two_quarters(i, carry):
        second = 2 * i + 1
        fill(second // 4, lax.rem(second, 4), taps_b, mix_b)
        gather(i // 2, taps_a, mix_a)
        third = jnp.minimum(2 * i + 2, 15)
        fill(third // 4, lax.rem(third, 4), taps_a, mix_a)
        gather(second // 4, taps_b, mix_b)
        return carry

    lax.fori_loop(0, 8, two_quarters, 0)

    own.wait()
    everyone = r.at[pl.ds(0, 63)]
    pltpu.make_async_copy(everyone, everyone, s3_recv).wait()
    block = lax.broadcasted_iota(jnp.int32, (32, 128), 1) // 32
    for quad in range(8):
        parts = [r[0:32, quad * 4 + i, :] + r[32:64, quad * 4 + i, :] for i in range(4)]
        turned = jnp.concatenate(parts, axis=0).T
        rows = [turned[a * 32 : a * 32 + 32, :] for a in range(4)]
        made = []
        for i in range(4):
            one = rows[i]
            for a in range(4):
                if a != i:
                    one = jnp.where(block == a, pltpu.roll(rows[a], ((a - i) * 32) % 128, 1), one)
            made.append(one)
        high, low = split(jnp.concatenate(made, axis=0))
        for n in range(2):
            order = ORDER_OF[quad * 2 + n]
            lhs[order, 0:64, :] = high[n * 64 : n * 64 + 64]
            lhs[order, 64:128, :] = low[n * 64 : n * 64 + 64]

    for copy in sends:
        copy.wait_send()
    for copy in edges:
        copy.wait_send()

    @pl.when(lat < 31)
    def _():
        for pair in halo:
            pair[0].wait_send()

    @pl.when(lat > 0)
    def _():
        for pair in halo:
            pair[1].wait_send()

    pltpu.make_async_copy(everyone, everyone, s3_send).wait()


def legendre_kernel(lhs, lp, conv, out, moved, made, out_sem, move_sem):
    moves = [pltpu.make_async_copy(conv.at[a], moved.at[:, a, :], move_sem.at[a]) for a in range(4)]
    for copy in moves:
        copy.start()

    def leaving(m):
        return pltpu.make_async_copy(made.at[m], out.at[m], out_sem.at[m])

    def order(m, carry):
        top, bottom = lhs[m, 0:64, :], lhs[m, 64:128, :]
        left = jnp.concatenate(
            [
                jnp.concatenate([top, top], axis=1),
                jnp.concatenate([bottom, jnp.zeros_like(bottom)], axis=1),
            ],
            axis=0,
        )
        both = jnp.dot(left, lp[m], preferred_element_type=F32)
        made[m] = both[0:64] + both[64:128]
        leaving(m).start()
        return carry

    lax.fori_loop(0, 16, order, 0, unroll=16)
    for copy in moves:
        copy.wait()
    lax.fori_loop(0, 16, lambda m, carry: leaving(m).wait(), None)


def shards(field, legendre, shifts, psi, kernel_weight):
    even, odd = fourier_tables()
    vmem = pl.BlockSpec(memory_space=pltpu.VMEM)
    hbm = pl.BlockSpec(memory_space=pltpu.HBM)
    dma = pltpu.SemaphoreType.DMA
    conv, lhs, prepared = pl.pallas_call(
        main_kernel,
        out_shape=(
            pltpu.VMEM((4, SLAB, 256), F32),
            pltpu.VMEM((16, 128, 128), BF16),
            pltpu.VMEM((16, 256, 720), BF16),
        ),
        in_specs=[hbm] * 7,
        out_specs=(vmem, vmem, vmem),
        scratch_shapes=[
            pltpu.VMEM((4, SLAB, 256), F32),
            pltpu.VMEM((2, 2, SLAB, 256), F32),
            pltpu.VMEM((2, 8, REACH, 256), F32),
            pltpu.VMEM((2, 2, 8, SPAN, 128), F32),
            pltpu.VMEM((8, PAD, 128), F32),
            pltpu.VMEM((2, 4, PAD, 128), F32),
            pltpu.VMEM((2, 32, 32, 128), F32),
            pltpu.VMEM((64, 32, 128), F32),
            pltpu.VMEM((2 * ROWS, STRIDE * 256), BF16),
            pltpu.VMEM((2 * ROWS, STRIDE * 256), BF16),
            pltpu.VMEM((2, STRIDE * 256, 256), BF16),
            pltpu.VMEM((2, STRIDE * 256, 256), BF16),
            pltpu.VMEM((2, 512, PAD), BF16),
            pltpu.VMEM((2, 512, 2 * PAD), BF16),
            pltpu.VMEM((2, 4, REACH, 256), F32),
            pltpu.VMEM((KERNELS, GW, 256), F32),
            pltpu.VMEM((16, 720, 128), F32),
            pltpu.VMEM((6, 128, 128), F32),
            pltpu.SMEM((4, SLOTS), jnp.int32),
            pltpu.SMEM((KERNELS, 4, SLOTS), F32),
            dma((4,)),
            dma((6,)),
            dma((2, 3)),
            dma((2, 3)),
            dma((2,)),
            dma((2,)),
            dma((3, 2)),
            dma((3, 2)),
            dma,
            dma,
            dma,
        ],
        compiler_params=pltpu.CompilerParams(
            collective_id=0, has_side_effects=True, vmem_limit_bytes=44 * 1024 * 1024
        ),
        cost_estimate=pl.CostEstimate(flops=4_000_000_000, bytes_accessed=8_000_000, transcendentals=0),
        name="spectrum_and_convolution",
    )(
        *(
            pltpu.with_memory_space_constraint(value, pltpu.HBM)
            for value in (
                shifts,
                psi.transpose(2, 0, 1),
                field.transpose(1, 0, 2),
                kernel_weight,
                jnp.asarray(even),
                jnp.asarray(odd),
                legendre,
            )
        )
    )
    coefficients, moved = pl.pallas_call(
        legendre_kernel,
        out_shape=(
            jax.ShapeDtypeStruct((16, 64, 720), F32),
            jax.ShapeDtypeStruct((SLAB, 4, 256), F32),
        ),
        in_specs=[vmem, vmem, vmem],
        out_specs=(hbm, hbm),
        scratch_shapes=[pltpu.VMEM((16, 64, 720), F32), dma((16,)), dma((4,))],
        compiler_params=pltpu.CompilerParams(vmem_limit_bytes=24 * 1024 * 1024),
        cost_estimate=pl.CostEstimate(flops=800_000_000, bytes_accessed=10_000_000, transcendentals=0),
        name="legendre",
    )(lhs, prepared, conv)
    coefficients = coefficients.reshape(16, 2, GW, 720).transpose(0, 3, 1, 2)
    return coefficients, moved.transpose(1, 0, 2)


def solution(mesh):
    placed = (
        P("lat", "lon", None),
        P("lat", None, None),
        P("lat", None),
        P("lat", None, None),
        P(),
    )
    return jax.shard_map(
        shards,
        mesh=mesh,
        in_specs=placed,
        out_specs=(P("lat", None, None, "lon"), P("lat", "lon", None)),
        check_vma=False,
    )
```
